512 devices in a mesh: replica: 32 (over z, x_hi, core), fsdp: 16 (over x_lo, y).
Axes of the slice: x: 4 (x_hi: 2, x_lo: 2; x = x_hi * 2 + x_lo), y: 8, z: 8, core: 2. Of those that a mesh axis runs over, the one named last changes fastest.
Arguments:
- tokens: bfloat16 [81920, 4608], P(('replica', 'fsdp')), may hold values from -8 to 8
- gain: float32 [32, 4608], P('replica'), may hold values from -0.5 to 0.5
- key_weight: bfloat16 [32, 4608, 1024], P('replica', 'fsdp'), may hold values from -2 to 2
- key_cotangent: bfloat16 [81920, 1024], P(('replica', 'fsdp')), may hold values from -6 to 6
- local_fragment: bfloat16 [32, 64, 4608], P('replica', 'fsdp'), may hold values from -6 to 6
- global_fragment: float32 [64, 4608], P('fsdp'), may hold values from -6 to 6
- outer_momentum: float32 [64, 4608], P('fsdp'), may hold values from -3 to 3
Outputs:
- keys: bfloat16 [81920, 1024], P(('replica', 'fsdp'))
- grad_tokens: bfloat16 [81920, 4608], P(('replica', 'fsdp'))
- grad_key_weight: bfloat16 [32, 4608, 1024], P('replica', 'fsdp')
- grad_gain: float32 [32, 4608], P('replica')
- new_global: float32 [64, 4608], P('fsdp')
- new_momentum: float32 [64, 4608], P('fsdp')
The draws below stay inside these ranges and needn't reach their ends.
All inputs are finite; a program needn't handle non-finite values.
Results may differ from the reference program's by a relative error of at most 0.0049.
Values may be sent and summed in bfloat16 or wider, within the bound.
A program may use at most 64 MiB of HBM per device.

```python
import math
import jax
import jax.numpy as jnp
from jax import lax

D = 4608
KV = 1024
FRAG_ROWS = 64
REPLICAS = 32
TOKENS = 81920
N_REPLICA = 32


def shared_part(key):
    return jnp.clip(jax.random.normal(key, (TOKENS, KV), jnp.float32), -4.0, 4.0)


def draw_tokens(key, part):
    shared = shared_part(key)
    key = jax.random.fold_in(key, 11)
    first = jax.random.fold_in(key, 0)
    rest = jnp.clip(jax.random.normal(first, (TOKENS, D - KV), jnp.float32), -4.0, 4.0)
    whole = jnp.concatenate([shared, rest], axis=1)
    return whole.astype(jnp.bfloat16)


def draw_key_cotangent(key, part):
    shared = shared_part(key)
    key = jax.random.fold_in(key, 12)
    noise = jnp.clip(jax.random.normal(key, (TOKENS, KV), jnp.float32), -4.0, 4.0)
    return (0.8 * shared + 0.6 * noise).astype(jnp.bfloat16)


def draw_key_weight(key, part):
    key = jax.random.fold_in(key, 13)
    noise = jnp.clip(jax.random.normal(key, (REPLICAS, D, KV), jnp.float32), -4.0, 4.0)
    diagonal = (jnp.arange(D)[:, None] == jnp.arange(KV)[None, :]).astype(jnp.float32)
    return (noise * (1.0 / math.sqrt(D)) + 0.7 * diagonal[None]).astype(jnp.bfloat16)


def block_scale(stream_key, dims, pieces, least, largest):
    level, own = 1.0, jax.random.fold_in(stream_key, 6)
    for axis_at, shards_of in pieces:
        steps = jnp.exp(jax.random.uniform(jax.random.fold_in(own, axis_at), (shards_of,), jnp.float32, least / len(pieces), largest / len(pieces)))
        level = level * jnp.repeat(steps, dims[axis_at] // shards_of).reshape([-1 if axis == axis_at else 1 for axis in range(len(dims))])
    return level


def gaussian(stream_key, dims, deviation, bound, shards=(), held_as=jnp.bfloat16):
    entries = deviation * jax.random.normal(stream_key, dims, jnp.float32)
    if shards:
        entries = entries * block_scale(stream_key, dims, shards, -0.22, 0.18)
    return jnp.clip(entries, -bound, bound).astype(held_as)


def setup_inputs(seed: int = 0) -> dict:
    seeds = jax.random.split(jax.random.key(seed), 8)
    return {
        "tokens": draw_tokens(jax.random.fold_in(seeds[7], 71), 0),
        "gain": jnp.clip(jax.random.uniform(seeds[1], (REPLICAS, D), jnp.float32, -0.5, 0.5) * block_scale(seeds[1], (REPLICAS, D), ((0, 32),), -0.4, 0.0), -0.5, 0.5),
        "key_weight": draw_key_weight(jax.random.fold_in(seeds[7], 71), 0),
        "key_cotangent": draw_key_cotangent(jax.random.fold_in(seeds[7], 71), 0),
        "local_fragment": gaussian(seeds[4], (REPLICAS, FRAG_ROWS, D), 1.0, 6.0, ((0, 32), (1, 16))),
        "global_fragment": gaussian(seeds[5], (FRAG_ROWS, D), 1.0, 6.0, ((0, 16),), jnp.float32),
        "outer_momentum": gaussian(seeds[6], (FRAG_ROWS, D), 0.5, 3.0, ((0, 16),), jnp.float32),
    }


eps = 1e-06

def one_replica(packed):
    rows, gain_row, weights, cotangent = packed
    xf = rows.astype(jnp.float32)
    rstd = lax.rsqrt(lax.optimization_barrier(jnp.mean(xf * xf, axis=-1, keepdims=True)) + eps)
    unit = xf * rstd
    scale = 1.0 + gain_row
    normed = (unit * scale).astype(jnp.bfloat16)
    keys = jnp.dot(normed, weights, preferred_element_type=jnp.float32).astype(jnp.bfloat16)
    grad_normed = jnp.dot(cotangent, weights.T, preferred_element_type=jnp.float32)
    grad_weight = jnp.dot(normed.T, cotangent, preferred_element_type=jnp.float32).astype(jnp.bfloat16)
    grad_gain = lax.optimization_barrier(jnp.sum(grad_normed * unit, axis=0))
    scaled = grad_normed * scale
    grad_rows = rstd * (scaled - unit * lax.optimization_barrier(jnp.mean(scaled * unit, axis=-1, keepdims=True)))
    return (keys, grad_rows.astype(jnp.bfloat16), grad_weight, grad_gain)

def reference(tokens, gain, key_weight, key_cotangent, local_fragment, global_fragment, outer_momentum):
    xs = tokens.reshape(N_REPLICA, -1, D)
    cots = key_cotangent.reshape(N_REPLICA, -1, KV)
    keys, grad_rows, grad_weight, grad_gain = lax.map(one_replica, (xs, gain, key_weight, cots))
    delta = global_fragment[None] - local_fragment.astype(jnp.float32)
    average = lax.optimization_barrier(jnp.sum(delta, axis=0)) / N_REPLICA
    new_momentum = 0.9 * outer_momentum + average
    new_global = global_fragment - 0.7 * (average + 0.9 * new_momentum)
    return (keys.reshape(-1, KV), grad_rows.reshape(-1, D), grad_weight, grad_gain, new_global, new_momentum)
```

```python
import functools

import jax
import jax.numpy as jnp
from jax import lax
from jax.experimental import pallas as pl
from jax.experimental.pallas import tpu as pltpu
from jax.sharding import PartitionSpec as P

eps = 1e-06
MESH = pl.DeviceIdType.MESH
f32, bf16 = jnp.float32, jnp.bfloat16

RING = 8
ROWS = 160
D = 4608
HALF = D // 2
KV = 1024
SHARD = 288
PIECE = SHARD // 2
HOPS = 7


def kernel(
    tok, gain, w, cot, frag, glob, mom,
    keys_o, gtok_o, gw_o, ggain_o, nglob_o, nmom_o,
    tokv, gainv, n2, nsend, c2, wall, part, rs_s, rs_r, dn_own, dn_s, dn_r, k_own, k_s, k_r,
    rstdv, gtokv, keysv, gwv, fragv, globv, momv, nglobv, nmomv,
    zring, zsum, core_r, csum, xhi_r, gring, gsum, gx_r, ggainv,
    ag_ss, ag_rs, rs_ss, rs_rs, x_ss, x_rs, z_ss, z_rs, g_ss, g_rs, h_ss, h_rs, loc,
):
    me = lax.axis_index("fsdp")
    rep = lax.axis_index("replica")
    x, y = me // RING, me % RING
    z, low = rep // 4, rep % 4
    core, xhi = low % 2, low // 2

    def fs(i):
        return {"fsdp": i}

    def rp(i):
        return {"replica": i}

    ring = (fs(x * RING + (y + 1) % RING), fs(x * RING + (y + RING - 1) % RING))
    zring_dev = (rp((z + 1) % RING * 4 + low), rp((z + RING - 1) % RING * 4 + low))
    partner = fs((1 - x) * RING + y)
    core_dev = rp(rep + 1 - 2 * core)
    xhi_dev = rp(rep + 2 - 4 * xhi)

    def local(i, src, dst):
        return pltpu.make_async_copy(src, dst, loc.at[i])

    def remote(src, dst, ss, rs, dev):
        return pltpu.make_async_remote_copy(
            src_ref=src, dst_ref=dst, send_sem=ss, recv_sem=rs, device_id=dev, device_id_type=MESH
        )

    own_rows = pl.ds(pl.multiple_of(y * SHARD, 16), SHARD)
    loads = [
        local(0, frag.at[0], fragv),
        local(1, tok, tokv),
        local(2, gain, gainv),
        local(3, cot, c2.at[pl.ds(0, ROWS)]),
        local(4, w.at[0], wall.at[own_rows]),
        local(5, glob, globv),
        local(6, mom, momv),
    ]
    for copy in loads:
        copy.start()

    barrier = pltpu.get_barrier_semaphore()
    peers = ring + zring_dev + (partner, core_dev, xhi_dev)
    for peer in peers:
        pl.semaphore_signal(barrier, inc=1, device_id=peer, device_id_type=MESH)
    pl.semaphore_wait(barrier, len(peers))

    def wpiece(direction, j, extra):
        away = j // 2 + extra
        shard = (y + RING - away) % RING if direction == 0 else (y + away) % RING
        half = (j % 2) ^ direction
        return wall.at[pl.ds(pl.multiple_of(shard * SHARD + half * PIECE, 16), PIECE)]

    def ag_copy(direction, j):
        there = wpiece(direction, j, 0)
        half = (j % 2) ^ direction
        src = w.at[0, pl.ds(half * PIECE, PIECE)] if j < 2 else there
        return remote(src, there, ag_ss.at[direction, j], ag_rs.at[direction, j], ring[direction])

    def ag_arrive(j):
        for direction in (0, 1):
            here = wpiece(direction, j, 1)
            remote(
                here, here, ag_ss.at[direction, j], ag_rs.at[direction, j], ring[direction]
            ).wait_recv()
            if j + 2 < HOPS:
                ag_copy(direction, j + 2).start()

    for j in (0, 1):
        for direction in (0, 1):
            ag_copy(direction, j).start()

    x_c = remote(cot, c2.at[pl.ds(ROWS, ROWS)], x_ss.at[0], x_rs.at[0], partner)
    x_n = remote(nsend, n2.at[pl.ds(ROWS, ROWS)], x_ss.at[1], x_rs.at[1], partner)
    x_dn = remote(dn_s, dn_r, x_ss.at[2], x_rs.at[2], partner)
    x_k = remote(k_s, k_r, x_ss.at[3], x_rs.at[3], partner)
    x_g = remote(gsum, gx_r, x_ss.at[4], x_rs.at[4], partner)
    x_c.start()

    def small_ring(buf, at, ss, rs, devs):
        def slot(direction, hop):
            return buf.at[(at + RING - hop) % RING if direction == 0 else (at + hop) % RING]

        def send(direction, hop):
            return remote(
                slot(direction, hop), slot(direction, hop),
                ss.at[direction, hop], rs.at[direction, hop], devs[direction],
            )

        def arrive(hop):
            for direction in (0, 1):
                if hop < 4 - direction:
                    here = slot(direction, hop + 1)
                    remote(
                        here, here, ss.at[direction, hop], rs.at[direction, hop], devs[direction]
                    ).wait_recv()
                    if hop + 1 < 4 - direction:
                        send(direction, hop + 1).start()

        return send, arrive

    z_send, z_arrive = small_ring(zring, z, z_ss, z_rs, zring_dev)
    g_send, g_arrive = small_ring(gring, y, g_ss, g_rs, ring)

    loads[0].wait()
    zring[z, pl.ds(0, 4)] = fragv[:, pl.ds(0, HALF)].astype(f32)
    zring[z, pl.ds(4, 4)] = fragv[:, pl.ds(HALF, HALF)].astype(f32)
    z_send(0, 0).start()
    z_send(1, 0).start()

    loads[1].wait()
    loads[2].wait()
    mine = x * HALF
    other = (1 - x) * HALF
    step = 768

    def cols(base, at):
        return pl.ds(pl.multiple_of(base + at, 128), step)

    def norm_block(i, _):
        rows = pl.ds(pl.multiple_of(i * 16, 16), 16)
        total = jnp.zeros((16, 128), f32)
        for at in range(0, D, step):
            v = tokv[rows, pl.ds(at, step)].astype(f32)
            v = v * v
            for k in range(0, step, 128):
                total = total + v[:, k : k + 128]
        mean = jnp.sum(total, axis=-1, keepdims=True) * (1.0 / D)
        rstd = lax.rsqrt(mean + eps)
        rstdv[rows, :] = jnp.broadcast_to(rstd, (16, 128))
        for base, to in ((other, nsend), (mine, n2)):
            for at in range(0, HALF, step):
                unit = tokv[rows, cols(base, at)].astype(f32) * rstd
                to[rows, pl.ds(at, step)] = (unit * (1.0 + gainv[:, cols(base, at)])).astype(bf16)
        return 0

    lax.fori_loop(0, ROWS // 16, norm_block, 0)
    x_n.start()

    ag_arrive(0)
    z_arrive(0)
    ag_arrive(1)
    z_arrive(1)
    ag_arrive(2)
    z_arrive(2)
    ag_arrive(3)
    z_arrive(3)

    loads[3].wait()
    x_c.wait_recv()
    x_n.wait_recv()

    def part_block(i, _):
        at = pl.multiple_of(i * 256, 256)
        part[pl.ds(at, 256), :] = lax.dot_general(
            n2[:, pl.ds(at, 256)], c2[...], (((0,), (0,)), ((), ())), preferred_element_type=f32
        )
        return 0

    lax.fori_loop(0, HALF // 256, part_block, 0)

    ag_arrive(4)

    def part_rows(direction, away, half, i):
        shard = (y + away) % RING if direction == 0 else (y + RING - away) % RING
        return pl.ds(pl.multiple_of(shard * SHARD + half * PIECE + i * 16, 16), 16)

    def rs_copy(direction, j):
        return remote(
            rs_s.at[direction, j], rs_r.at[direction, j],
            rs_ss.at[direction, j], rs_rs.at[direction, j], ring[direction],
        )

    def rs_send(direction, j):
        half, away = (j % 2) ^ direction, 4 - (j + 1) // 2

        def block(i, _):
            rows = pl.ds(pl.multiple_of(i * 16, 16), 16)
            v = part[part_rows(direction, away, half, i), :]
            if j >= 2:
                v = v + rs_r[direction, j - 2, rows, :].astype(f32)
            rs_s[direction, j, rows, :] = v.astype(bf16)
            return 0

        lax.fori_loop(0, PIECE // 16, block, 0)
        rs_copy(direction, j).start()

    def rs_arrive(j):
        for direction in (0, 1):
            rs_copy(direction, j).wait_recv()
            if j + 2 < HOPS:
                rs_send(direction, j + 2)

    for j in (0, 1):
        for direction in (0, 1):
            rs_send(direction, j)

    total = zring[0]
    for k in range(1, RING):
        total = total + zring[k]
    zsum[...] = total
    x_core = remote(zsum, core_r, h_ss.at[0], h_rs.at[0], core_dev)
    x_xhi = remote(csum, xhi_r, h_ss.at[1], h_rs.at[1], xhi_dev)
    x_core.start()

    ag_arrive(5)
    x_core.wait_recv()
    csum[...] = zsum[...] + core_r[...]
    x_xhi.start()
    ag_arrive(6)
    loads[4].wait()

    def dn_block(i, _):
        at = pl.multiple_of(i * 256, 256)
        v = lax.dot_general(
            c2[...], wall[pl.ds(at, 256), :], (((1,), (1,)), ((), ())), preferred_element_type=f32
        )
        dn_own[:, pl.ds(at, 256)] = v[:ROWS]
        dn_s[:, pl.ds(at, 256)] = v[ROWS:].astype(bf16)
        gring[y, :, pl.ds(at, 256)] = jnp.sum(
            v * n2[:, pl.ds(at, 256)].astype(f32), axis=0, keepdims=True
        )
        return 0

    lax.fori_loop(0, HALF // 256, dn_block, 0)
    x_dn.start()
    g_send(0, 0).start()
    g_send(1, 0).start()

    def key_block(i, _):
        at = pl.multiple_of(i * 256, 256)
        v = jnp.dot(n2[...], wall[:, pl.ds(at, 256)], preferred_element_type=f32)
        k_own[:, pl.ds(at, 256)] = v[:ROWS]
        k_s[:, pl.ds(at, 256)] = v[ROWS:].astype(bf16)
        return 0

    lax.fori_loop(0, KV // 256, key_block, 0)
    x_k.start()

    rs_arrive(0)
    g_arrive(0)

    loads[5].wait()
    loads[6].wait()
    x_xhi.wait_recv()
    for k in (0, 1):
        here = pl.ds(k * HALF, HALF)
        locals_sum = csum[pl.ds(4 * k, 4), :] + xhi_r[pl.ds(4 * k, 4), :]
        g = globv[:, here]
        average = (32.0 * g - locals_sum) * (1.0 / 32.0)
        momentum = 0.9 * momv[:, here] + average
        nmomv[:, here] = momentum
        nglobv[:, here] = g - 0.7 * (average + 0.9 * momentum)
    stores = [local(7, nglobv, nglob_o), local(8, nmomv, nmom_o)]
    for copy in stores:
        copy.start()

    rs_arrive(1)
    g_arrive(1)
    rs_arrive(2)
    g_arrive(2)
    rs_arrive(3)
    g_arrive(3)

    total = gring[0]
    for k in range(1, RING):
        total = total + gring[k]
    gsum[...] = total / (1.0 + gainv[:, pl.ds(pl.multiple_of(mine, 128), HALF)])
    x_g.start()

    x_k.wait_recv()

    def keys_block(i, _):
        rows = pl.ds(pl.multiple_of(i * 16, 16), 16)
        keysv[rows, :] = (k_own[rows, :] + k_r[rows, :].astype(f32)).astype(bf16)
        return 0

    lax.fori_loop(0, ROWS // 16, keys_block, 0)
    store = local(9, keysv, keys_o)
    store.start()
    stores.append(store)

    x_dn.wait_recv()
    rs_arrive(4)

    def gtok_block(i, _):
        rows = pl.ds(pl.multiple_of(i * 16, 16), 16)
        rstd = rstdv[rows, pl.ds(0, 1)]
        total = jnp.zeros((16, 128), f32)
        for base, grad in ((mine, dn_own), (other, dn_r)):
            for at in range(0, HALF, step):
                unit = tokv[rows, cols(base, at)].astype(f32) * rstd
                scaled = grad[rows, pl.ds(at, step)].astype(f32) * (1.0 + gainv[:, cols(base, at)])
                v = scaled * unit
                for k in range(0, step, 128):
                    total = total + v[:, k : k + 128]
        mean = jnp.sum(total, axis=-1, keepdims=True) * (1.0 / D)
        for base, grad in ((mine, dn_own), (other, dn_r)):
            for at in range(0, HALF, step):
                unit = tokv[rows, cols(base, at)].astype(f32) * rstd
                scaled = grad[rows, pl.ds(at, step)].astype(f32) * (1.0 + gainv[:, cols(base, at)])
                gtokv[rows, cols(base, at)] = (rstd * (scaled - unit * mean)).astype(bf16)
        return 0

    lax.fori_loop(0, ROWS // 16, gtok_block, 0)
    store = local(10, gtokv, gtok_o)
    store.start()
    stores.append(store)

    x_g.wait_recv()
    ggainv[:, pl.ds(pl.multiple_of(mine, 128), HALF)] = gsum[...]
    ggainv[:, pl.ds(pl.multiple_of(other, 128), HALF)] = gx_r[...]
    store = local(11, ggainv, ggain_o)
    store.start()
    stores.append(store)

    rs_arrive(5)

    def early_block(direction):
        half = 1 - direction

        def block(i, _):
            rows = part_rows(0, 0, half, i)
            arrived = rs_r[direction, 5, pl.ds(pl.multiple_of(i * 16, 16), 16), :]
            part[rows, :] = part[rows, :] + arrived.astype(f32)
            return 0

        return block

    for direction in (0, 1):
        lax.fori_loop(0, PIECE // 16, early_block(direction), 0)
    rs_arrive(6)

    def last_block(direction):
        half = direction

        def block(i, _):
            arrived = rs_r[direction, 6, pl.ds(pl.multiple_of(i * 16, 16), 16), :]
            to = pl.ds(pl.multiple_of(half * PIECE + i * 16, 16), 16)
            v = part[part_rows(0, 0, half, i), :] + arrived.astype(f32)
            gwv[to, :] = v.astype(bf16)
            return 0

        return block

    for direction in (0, 1):
        lax.fori_loop(0, PIECE // 16, last_block(direction), 0)
    store = local(12, gwv, gw_o.at[0])
    store.start()
    stores.append(store)

    for direction in (0, 1):
        for j in range(HOPS):
            ag_copy(direction, j).wait_send()
            rs_copy(direction, j).wait_send()
        for hop in range(4 - direction):
            z_send(direction, hop).wait_send()
            g_send(direction, hop).wait_send()
    for copy in (x_c, x_n, x_dn, x_k, x_g, x_core, x_xhi):
        copy.wait_send()
    for copy in stores:
        copy.wait()


def on_device(tokens, gain, key_weight, key_cotangent, local_fragment, global_fragment, outer_momentum):
    v, dma = pltpu.VMEM, pltpu.SemaphoreType.DMA
    return pl.pallas_call(
        kernel,
        out_shape=(
            jax.ShapeDtypeStruct((ROWS, KV), bf16),
            jax.ShapeDtypeStruct((ROWS, D), bf16),
            jax.ShapeDtypeStruct((1, SHARD, KV), bf16),
            jax.ShapeDtypeStruct((1, D), f32),
            jax.ShapeDtypeStruct((4, D), f32),
            jax.ShapeDtypeStruct((4, D), f32),
        ),
        in_specs=[pl.BlockSpec(memory_space=pl.ANY)] * 7,
        out_specs=[pl.BlockSpec(memory_space=pl.ANY)] * 6,
        scratch_shapes=[
            v((ROWS, D), bf16),
            v((1, D), f32),
            v((2 * ROWS, HALF), bf16),
            v((ROWS, HALF), bf16),
            v((2 * ROWS, KV), bf16),
            v((HALF, KV), bf16),
            v((HALF, KV), f32),
            v((2, HOPS, PIECE, KV), bf16),
            v((2, HOPS, PIECE, KV), bf16),
            v((ROWS, HALF), f32),
            v((ROWS, HALF), bf16),
            v((ROWS, HALF), bf16),
            v((ROWS, KV), f32),
            v((ROWS, KV), bf16),
            v((ROWS, KV), bf16),
            v((ROWS, 128), f32),
            v((ROWS, D), bf16),
            v((ROWS, KV), bf16),
            v((SHARD, KV), bf16),
            v((4, D), bf16),
            v((4, D), f32),
            v((4, D), f32),
            v((4, D), f32),
            v((4, D), f32),
            v((RING, 8, HALF), f32),
            v((8, HALF), f32),
            v((8, HALF), f32),
            v((8, HALF), f32),
            v((8, HALF), f32),
            v((RING, 1, HALF), f32),
            v((1, HALF), f32),
            v((1, HALF), f32),
            v((1, D), f32),
            dma((2, HOPS)),
            dma((2, HOPS)),
            dma((2, HOPS)),
            dma((2, HOPS)),
            dma((5,)),
            dma((5,)),
            dma((2, 4)),
            dma((2, 4)),
            dma((2, 4)),
            dma((2, 4)),
            dma((2,)),
            dma((2,)),
            dma((13,)),
        ],
        compiler_params=pltpu.CompilerParams(
            collective_id=0, has_side_effects=True, vmem_limit_bytes=52 * 2**20
        ),
        cost_estimate=pl.CostEstimate(
            flops=6 * ROWS * D * KV, bytes_accessed=8 * 2**20, transcendentals=ROWS
        ),
    )(tokens, gain, key_weight, key_cotangent, local_fragment, global_fragment, outer_momentum)


def solution(mesh):
    placed = (
        P(("replica", "fsdp"), None),
        P("replica", None),
        P("replica", "fsdp", None),
        P(("replica", "fsdp"), None),
        P("replica", "fsdp", None),
        P("fsdp", None),
        P("fsdp", None),
    )
    return jax.shard_map(
        on_device,
        mesh=mesh,
        in_specs=placed,
        out_specs=(
            P(("replica", "fsdp"), None),
            P(("replica", "fsdp"), None),
            P("replica", "fsdp", None),
            P("replica", None),
            P("fsdp", None),
            P("fsdp", None),
        ),
        check_vma=False,
    )
```

```python
import functools

import jax
import jax.numpy as jnp
from jax import lax
from jax.experimental import pallas as pl
from jax.experimental.pallas import tpu as pltpu
from jax.sharding import PartitionSpec as P

eps = 1e-06
MESH = pl.DeviceIdType.MESH
f32, bf16 = jnp.float32, jnp.bfloat16

RING = 8
ROWS = 160
D = 4608
HALF = D // 2
KV = 1024
SHARD = 288
PIECE = SHARD // 2
HOPS = 7


def kernel(
    tok, gain, w, cot, frag, glob, mom,
    keys_o, gtok_o, gw_o, ggain_o, nglob_o, nmom_o,
    tokv, gainv, n2, nsend, c2, wall, part, rs_s, rs_r, dn_own, dn_s, dn_r, k_own, k_s, k_r,
    rstdv, gtokv, keysv, gwv, fragv, globv, momv, nglobv, nmomv,
    zacc, zin_r, core_r, csum, xhi_r, ztotal, gring, gsum, gx_r, ggainv,
    ag_ss, ag_rs, rs_ss, rs_rs, x_ss, x_rs, z_ss, z_rs, g_ss, g_rs, above_in, loc,
):
    me = lax.axis_index("fsdp")
    rep = lax.axis_index("replica")
    x, y = me // RING, me % RING
    z, low = rep // 4, rep % 4
    core, xhi = low % 2, low // 2

    def fs(i):
        return {"fsdp": i}

    def rp(i):
        return {"replica": i}

    ring = (fs(x * RING + (y + 1) % RING), fs(x * RING + (y + RING - 1) % RING))
    last = RING - 1
    above, below = rp((z + 1) % RING * 4 + low), rp((z + last) % RING * 4 + low)
    partner = fs((1 - x) * RING + y)
    core_dev = rp(rep + 1 - 2 * core)
    xhi_dev = rp(rep + 2 - 4 * xhi)

    def local(i, src, dst):
        return pltpu.make_async_copy(src, dst, loc.at[i])

    def remote(src, dst, ss, rs, dev):
        return pltpu.make_async_remote_copy(
            src_ref=src, dst_ref=dst, send_sem=ss, recv_sem=rs, device_id=dev, device_id_type=MESH
        )

    own_rows = pl.ds(pl.multiple_of(y * SHARD, 16), SHARD)
    loads = [
        local(0, frag.at[0], fragv),
        local(1, tok, tokv),
        local(2, gain, gainv),
        local(3, cot, c2.at[pl.ds(0, ROWS)]),
        local(4, w.at[0], wall.at[own_rows]),
        local(5, glob, globv),
        local(6, mom, momv),
    ]
    for copy in loads:
        copy.start()

    barrier = pltpu.get_barrier_semaphore()

    def greet(peer):
        pl.semaphore_signal(barrier, inc=1, device_id=peer, device_id_type=MESH)

    for peer in ring + (partner,):
        greet(peer)

    @pl.when(z < last)
    def _():
        greet(above)

    @pl.when(z == last)
    def _():
        greet(core_dev)
        greet(xhi_dev)

    greeted = 3 + jnp.where(z > 0, 1, 0) + jnp.where(z == last, 2, 0)
    pl.semaphore_wait(barrier, greeted)

    @pl.when(z > 0)
    def _():
        pl.semaphore_signal(above_in, inc=1, device_id=below, device_id_type=MESH)

    def wpiece(direction, j, extra):
        away = j // 2 + extra
        shard = (y + RING - away) % RING if direction == 0 else (y + away) % RING
        half = (j % 2) ^ direction
        return wall.at[pl.ds(pl.multiple_of(shard * SHARD + half * PIECE, 16), PIECE)]

    def ag_copy(direction, j):
        there = wpiece(direction, j, 0)
        half = (j % 2) ^ direction
        src = w.at[0, pl.ds(half * PIECE, PIECE)] if j < 2 else there
        return remote(src, there, ag_ss.at[direction, j], ag_rs.at[direction, j], ring[direction])

    def ag_arrive(j):
        for direction in (0, 1):
            here = wpiece(direction, j, 1)
            remote(
                here, here, ag_ss.at[direction, j], ag_rs.at[direction, j], ring[direction]
            ).wait_recv()
            if j + 2 < HOPS:
                ag_copy(direction, j + 2).start()

    for j in (0, 1):
        for direction in (0, 1):
            ag_copy(direction, j).start()

    x_c = remote(c2.at[pl.ds(0, ROWS)], c2.at[pl.ds(ROWS, ROWS)], x_ss.at[0], x_rs.at[0], partner)
    x_n = remote(nsend, n2.at[pl.ds(ROWS, ROWS)], x_ss.at[1], x_rs.at[1], partner)
    x_dn = remote(dn_s, dn_r, x_ss.at[2], x_rs.at[2], partner)
    x_k = remote(k_s, k_r, x_ss.at[3], x_rs.at[3], partner)
    x_g = remote(gsum, gx_r, x_ss.at[4], x_rs.at[4], partner)
    loads[3].wait()
    x_c.start()

    def small_ring(buf, at, ss, rs, devs):
        def slot(direction, hop):
            return buf.at[(at + RING - hop) % RING if direction == 0 else (at + hop) % RING]

        def send(direction, hop):
            return remote(
                slot(direction, hop), slot(direction, hop),
                ss.at[direction, hop], rs.at[direction, hop], devs[direction],
            )

        def arrive(hop):
            for direction in (0, 1):
                if hop < 4 - direction:
                    here = slot(direction, hop + 1)
                    remote(
                        here, here, ss.at[direction, hop], rs.at[direction, hop], devs[direction]
                    ).wait_recv()
                    if hop + 1 < 4 - direction:
                        send(direction, hop + 1).start()

        return send, arrive

    g_send, g_arrive = small_ring(gring, y, g_ss, g_rs, ring)

    z_up = remote(zacc, zin_r, z_ss.at[0], z_rs.at[0], above)
    z_core = remote(zacc, core_r, z_ss.at[1], z_rs.at[1], core_dev)
    z_xhi = remote(csum, xhi_r, z_ss.at[2], z_rs.at[2], xhi_dev)
    z_down = remote(ztotal, ztotal, z_ss.at[3], z_rs.at[3], below)

    def z_rise(low, high):
        @pl.when((z >= low) & (z <= high))
        def _():
            if low > 0:
                z_up.wait_recv()
                zacc[...] = zacc[...] + zin_r[...]
            if high < last:
                pl.semaphore_wait(above_in, 1)
                z_up.start()

        if high == last:

            @pl.when(z == last)
            def _():
                z_core.start()

    def z_turn_core():
        @pl.when(z == last)
        def _():
            z_core.wait_recv()
            csum[...] = zacc[...] + core_r[...]
            z_xhi.start()

    def z_turn_x():
        @pl.when(z == last)
        def _():
            z_xhi.wait_recv()
            ztotal[...] = csum[...] + xhi_r[...]
            z_down.start()

    def z_fall(at):
        @pl.when(z == at)
        def _():
            z_down.wait_recv()
            if at > 0:
                z_down.start()

    loads[0].wait()
    zacc[pl.ds(0, 4), :] = fragv[:, pl.ds(0, HALF)].astype(f32)
    zacc[pl.ds(4, 4), :] = fragv[:, pl.ds(HALF, HALF)].astype(f32)

    loads[1].wait()
    loads[2].wait()
    mine = x * HALF
    other = (1 - x) * HALF
    step = 768

    def cols(base, at):
        return pl.ds(pl.multiple_of(base + at, 128), step)

    def norm_block(i, _):
        rows = pl.ds(pl.multiple_of(i * 16, 16), 16)
        total = jnp.zeros((16, 128), f32)
        for at in range(0, D, step):
            v = tokv[rows, pl.ds(at, step)].astype(f32)
            v = v * v
            for k in range(0, step, 128):
                total = total + v[:, k : k + 128]
        mean = jnp.sum(total, axis=-1, keepdims=True) * (1.0 / D)
        rstd = lax.rsqrt(mean + eps)
        rstdv[rows, :] = jnp.broadcast_to(rstd, (16, 128))
        for base, to in ((other, nsend), (mine, n2)):
            for at in range(0, HALF, step):
                unit = tokv[rows, cols(base, at)].astype(f32) * rstd
                to[rows, pl.ds(at, step)] = (unit * (1.0 + gainv[:, cols(base, at)])).astype(bf16)
        return 0

    lax.fori_loop(0, ROWS // 16, norm_block, 0)
    x_n.start()
    z_rise(0, 0)

    ag_arrive(0)
    z_rise(1, 2)
    ag_arrive(1)
    z_rise(3, 4)
    ag_arrive(2)
    z_rise(5, 6)
    z_rise(7, 7)
    ag_arrive(3)
    z_turn_core()

    x_c.wait_recv()
    x_n.wait_recv()

    def part_block(i, _):
        at = pl.multiple_of(i * 256, 256)
        part[pl.ds(at, 256), :] = lax.dot_general(
            n2[:, pl.ds(at, 256)], c2[...], (((0,), (0,)), ((), ())), preferred_element_type=f32
        )
        return 0

    lax.fori_loop(0, HALF // 256, part_block, 0)

    ag_arrive(4)
    z_turn_x()

    def part_rows(direction, away, half, i):
        shard = (y + away) % RING if direction == 0 else (y + RING - away) % RING
        return pl.ds(pl.multiple_of(shard * SHARD + half * PIECE + i * 16, 16), 16)

    def rs_copy(direction, j):
        return remote(
            rs_s.at[direction, j], rs_r.at[direction, j],
            rs_ss.at[direction, j], rs_rs.at[direction, j], ring[direction],
        )

    def rs_send(direction, j):
        half, away = (j % 2) ^ direction, 4 - (j + 1) // 2

        def block(i, _):
            rows = pl.ds(pl.multiple_of(i * 16, 16), 16)
            v = part[part_rows(direction, away, half, i), :]
            if j >= 2:
                v = v + rs_r[direction, j - 2, rows, :].astype(f32)
            rs_s[direction, j, rows, :] = v.astype(bf16)
            return 0

        lax.fori_loop(0, PIECE // 16, block, 0)
        rs_copy(direction, j).start()

    def rs_arrive(j):
        for direction in (0, 1):
            rs_copy(direction, j).wait_recv()
            if j + 2 < HOPS:
                rs_send(direction, j + 2)

    for j in (0, 1):
        for direction in (0, 1):
            rs_send(direction, j)

    ag_arrive(5)
    z_fall(6)
    ag_arrive(6)
    z_fall(5)
    loads[4].wait()

    def dn_block(i, _):
        at = pl.multiple_of(i * 256, 256)
        v = lax.dot_general(
            c2[...], wall[pl.ds(at, 256), :], (((1,), (1,)), ((), ())), preferred_element_type=f32
        )
        dn_own[:, pl.ds(at, 256)] = v[:ROWS]
        dn_s[:, pl.ds(at, 256)] = v[ROWS:].astype(bf16)
        gring[y, :, pl.ds(at, 256)] = jnp.sum(
            v * n2[:, pl.ds(at, 256)].astype(f32), axis=0, keepdims=True
        )
        return 0

    lax.fori_loop(0, HALF // 256, dn_block, 0)
    x_dn.start()
    g_send(0, 0).start()
    g_send(1, 0).start()

    def key_block(i, _):
        at = pl.multiple_of(i * 256, 256)
        v = jnp.dot(n2[...], wall[:, pl.ds(at, 256)], preferred_element_type=f32)
        k_own[:, pl.ds(at, 256)] = v[:ROWS]
        k_s[:, pl.ds(at, 256)] = v[ROWS:].astype(bf16)
        return 0

    lax.fori_loop(0, KV // 256, key_block, 0)
    x_k.start()

    rs_arrive(0)
    z_fall(4)
    g_arrive(0)

    rs_arrive(1)
    z_fall(3)
    g_arrive(1)
    rs_arrive(2)
    z_fall(2)
    g_arrive(2)
    rs_arrive(3)
    z_fall(1)
    g_arrive(3)

    stores = []

    total = gring[0]
    for k in range(1, RING):
        total = total + gring[k]
    gsum[...] = total / (1.0 + gainv[:, pl.ds(pl.multiple_of(mine, 128), HALF)])
    x_g.start()

    x_k.wait_recv()

    def keys_block(i, _):
        rows = pl.ds(pl.multiple_of(i * 16, 16), 16)
        keysv[rows, :] = (k_own[rows, :] + k_r[rows, :].astype(f32)).astype(bf16)
        return 0

    lax.fori_loop(0, ROWS // 16, keys_block, 0)
    store = local(9, keysv, keys_o)
    store.start()
    stores.append(store)

    x_dn.wait_recv()
    rs_arrive(4)
    z_fall(0)

    def gtok_block(i, _):
        rows = pl.ds(pl.multiple_of(i * 16, 16), 16)
        rstd = rstdv[rows, pl.ds(0, 1)]
        total = jnp.zeros((16, 128), f32)
        for base, grad in ((mine, dn_own), (other, dn_r)):
            for at in range(0, HALF, step):
                unit = tokv[rows, cols(base, at)].astype(f32) * rstd
                scaled = grad[rows, pl.ds(at, step)].astype(f32) * (1.0 + gainv[:, cols(base, at)])
                v = scaled * unit
                for k in range(0, step, 128):
                    total = total + v[:, k : k + 128]
        mean = jnp.sum(total, axis=-1, keepdims=True) * (1.0 / D)
        for base, grad in ((mine, dn_own), (other, dn_r)):
            for at in range(0, HALF, step):
                unit = tokv[rows, cols(base, at)].astype(f32) * rstd
                scaled = grad[rows, pl.ds(at, step)].astype(f32) * (1.0 + gainv[:, cols(base, at)])
                gtokv[rows, cols(base, at)] = (rstd * (scaled - unit * mean)).astype(bf16)
        return 0

    lax.fori_loop(0, ROWS // 16, gtok_block, 0)
    store = local(10, gtokv, gtok_o)
    store.start()
    stores.append(store)

    loads[5].wait()
    loads[6].wait()
    for k in (0, 1):
        here = pl.ds(k * HALF, HALF)
        locals_sum = ztotal[pl.ds(4 * k, 4), :]
        g = globv[:, here]
        average = (32.0 * g - locals_sum) * (1.0 / 32.0)
        momentum = 0.9 * momv[:, here] + average
        nmomv[:, here] = momentum
        nglobv[:, here] = g - 0.7 * (average + 0.9 * momentum)
    for copy in (local(7, nglobv, nglob_o), local(8, nmomv, nmom_o)):
        copy.start()
        stores.append(copy)

    x_g.wait_recv()
    ggainv[:, pl.ds(pl.multiple_of(mine, 128), HALF)] = gsum[...]
    ggainv[:, pl.ds(pl.multiple_of(other, 128), HALF)] = gx_r[...]
    store = local(11, ggainv, ggain_o)
    store.start()
    stores.append(store)

    rs_arrive(5)

    def early_block(direction):
        half = 1 - direction

        def block(i, _):
            rows = part_rows(0, 0, half, i)
            arrived = rs_r[direction, 5, pl.ds(pl.multiple_of(i * 16, 16), 16), :]
            part[rows, :] = part[rows, :] + arrived.astype(f32)
            return 0

        return block

    for direction in (0, 1):
        lax.fori_loop(0, PIECE // 16, early_block(direction), 0)
    rs_arrive(6)

    def last_block(direction):
        half = direction

        def block(i, _):
            arrived = rs_r[direction, 6, pl.ds(pl.multiple_of(i * 16, 16), 16), :]
            to = pl.ds(pl.multiple_of(half * PIECE + i * 16, 16), 16)
            v = part[part_rows(0, 0, half, i), :] + arrived.astype(f32)
            gwv[to, :] = v.astype(bf16)
            return 0

        return block

    for direction in (0, 1):
        lax.fori_loop(0, PIECE // 16, last_block(direction), 0)
    store = local(12, gwv, gw_o.at[0])
    store.start()
    stores.append(store)

    for direction in (0, 1):
        for j in range(HOPS):
            ag_copy(direction, j).wait_send()
            rs_copy(direction, j).wait_send()
        for hop in range(4 - direction):
            g_send(direction, hop).wait_send()
    for copy in (x_c, x_n, x_dn, x_k, x_g):
        copy.wait_send()

    @pl.when(z < last)
    def _():
        z_up.wait_send()

    @pl.when(z == last)
    def _():
        z_core.wait_send()
        z_xhi.wait_send()

    @pl.when(z > 0)
    def _():
        z_down.wait_send()

    for copy in stores:
        copy.wait()


def hand_over(*refs):
    sources, results, staged, sems = refs[:6], refs[6:12], refs[12:18], refs[18]
    order = range(6)
    ins = [pltpu.make_async_copy(sources[i], staged[i], sems.at[0, i]) for i in order]
    outs = [pltpu.make_async_copy(staged[i], results[i], sems.at[1, i]) for i in order]
    for copy in ins:
        copy.start()
    for i in order:
        ins[i].wait()
        outs[i].start()
    for copy in outs:
        copy.wait()


def on_device(tokens, gain, key_weight, key_cotangent, local_fragment, global_fragment, outer_momentum):
    v, dma = pltpu.VMEM, pltpu.SemaphoreType.DMA
    hbm, anywhere = pl.BlockSpec(memory_space=pltpu.HBM), pl.BlockSpec(memory_space=pl.ANY)
    shapes = (
        jax.ShapeDtypeStruct((ROWS, KV), bf16),
        jax.ShapeDtypeStruct((ROWS, D), bf16),
        jax.ShapeDtypeStruct((1, SHARD, KV), bf16),
        jax.ShapeDtypeStruct((1, D), f32),
        jax.ShapeDtypeStruct((4, D), f32),
        jax.ShapeDtypeStruct((4, D), f32),
    )
    outs = pl.pallas_call(
        kernel,
        out_shape=shapes,
        in_specs=[hbm] * 7,
        out_specs=[anywhere] * 6,
        scratch_shapes=[
            v((ROWS, D), bf16),
            v((1, D), f32),
            v((2 * ROWS, HALF), bf16),
            v((ROWS, HALF), bf16),
            v((2 * ROWS, KV), bf16),
            v((HALF, KV), bf16),
            v((HALF, KV), f32),
            v((2, HOPS, PIECE, KV), bf16),
            v((2, HOPS, PIECE, KV), bf16),
            v((ROWS, HALF), f32),
            v((ROWS, HALF), bf16),
            v((ROWS, HALF), bf16),
            v((ROWS, KV), f32),
            v((ROWS, KV), bf16),
            v((ROWS, KV), bf16),
            v((ROWS, 128), f32),
            v((ROWS, D), bf16),
            v((ROWS, KV), bf16),
            v((SHARD, KV), bf16),
            v((4, D), bf16),
            v((4, D), f32),
            v((4, D), f32),
            v((4, D), f32),
            v((4, D), f32),
            v((8, HALF), f32),
            v((8, HALF), f32),
            v((8, HALF), f32),
            v((8, HALF), f32),
            v((8, HALF), f32),
            v((8, HALF), f32),
            v((RING, 1, HALF), f32),
            v((1, HALF), f32),
            v((1, HALF), f32),
            v((1, D), f32),
            dma((2, HOPS)),
            dma((2, HOPS)),
            dma((2, HOPS)),
            dma((2, HOPS)),
            dma((5,)),
            dma((5,)),
            dma((4,)),
            dma((4,)),
            dma((2, 4)),
            dma((2, 4)),
            pltpu.SemaphoreType.REGULAR,
            dma((13,)),
        ],
        compiler_params=pltpu.CompilerParams(
            collective_id=0, has_side_effects=True, vmem_limit_bytes=63 * 2**20
        ),
        cost_estimate=pl.CostEstimate(
            flops=6 * ROWS * D * KV, bytes_accessed=8 * 2**20, transcendentals=ROWS
        ),
    )(tokens, gain, key_weight, key_cotangent, local_fragment, global_fragment, outer_momentum)
    return pl.pallas_call(
        hand_over,
        out_shape=shapes,
        in_specs=[anywhere] * 6,
        out_specs=[hbm] * 6,
        scratch_shapes=[v(s.shape, s.dtype) for s in shapes] + [dma((2, 6))],
    )(*outs)


def solution(mesh):
    placed = (
        P(("replica", "fsdp"), None),
        P("replica", None),
        P("replica", "fsdp", None),
        P(("replica", "fsdp"), None),
        P("replica", "fsdp", None),
        P("fsdp", None),
        P("fsdp", None),
    )
    return jax.shard_map(
        on_device,
        mesh=mesh,
        in_specs=placed,
        out_specs=(
            P(("replica", "fsdp"), None),
            P(("replica", "fsdp"), None),
            P("replica", "fsdp", None),
            P("replica", None),
            P("fsdp", None),
            P("fsdp", None),
        ),
        check_vma=False,
    )
```

```python
import functools

import jax
import jax.numpy as jnp
from jax import lax
from jax.experimental import pallas as pl
from jax.experimental.pallas import tpu as pltpu
from jax.sharding import PartitionSpec as P

eps = 1e-06
MESH = pl.DeviceIdType.MESH
f32, bf16 = jnp.float32, jnp.bfloat16

RING = 8
ROWS = 160
D = 4608
HALF = D // 2
KV = 1024
SHARD = 288
PIECE = SHARD // 2
HOPS = 7
CUTS = 3
CUT = PIECE // CUTS


def kernel(
    tok, gain, w, cot, frag, glob, mom,
    keys_o, gtok_o, gw_o, ggain_o, nglob_o, nmom_o,
    tokv, gainv, n2, nsend, c2, wall, part, rs_s, rs_r, dn_own, dn_s, dn_r, k_own, k_s, k_r,
    rstdv, fragv, globv, momv,
    zacc, zin_r, core_r, csum, xhi_r, ztotal, gring, gsum, gx_r,
    ag_ss, ag_rs, rs_ss, rs_rs, x_ss, x_rs, z_ss, z_rs, g_ss, g_rs, above_in, partner_in, core_in, xhi_in, loc,
):
    me = lax.axis_index("fsdp")
    rep = lax.axis_index("replica")
    x, y = me // RING, me % RING
    z, low = rep // 4, rep % 4
    core, xhi = low % 2, low // 2

    def fs(i):
        return {"fsdp": i}

    def rp(i):
        return {"replica": i}

    ring = (fs(x * RING + (y + 1) % RING), fs(x * RING + (y + RING - 1) % RING))
    last = RING - 1
    above, below = rp((z + 1) % RING * 4 + low), rp((z + last) % RING * 4 + low)
    partner = fs((1 - x) * RING + y)
    core_dev = rp(rep + 1 - 2 * core)
    xhi_dev = rp(rep + 2 - 4 * xhi)

    def local(i, src, dst):
        return pltpu.make_async_copy(src, dst, loc.at[i])

    def remote(src, dst, ss, rs, dev):
        return pltpu.make_async_remote_copy(
            src_ref=src, dst_ref=dst, send_sem=ss, recv_sem=rs, device_id=dev, device_id_type=MESH
        )

    own_rows = pl.ds(pl.multiple_of(y * SHARD, 16), SHARD)
    loads = [
        local(0, frag.at[0], fragv),
        local(1, tok, tokv),
        local(2, gain, gainv),
        local(3, cot, c2.at[pl.ds(0, ROWS)]),
        local(4, w.at[0], wall.at[own_rows]),
        local(5, glob, globv),
        local(6, mom, momv),
    ]

    barrier = pltpu.get_barrier_semaphore()

    def greet(peer):
        pl.semaphore_signal(barrier, inc=1, device_id=peer, device_id_type=MESH)

    for peer in ring:
        greet(peer)

    at_top = z == last
    pairs = (
        (True, x == 0, partner, partner_in),
        (at_top, core == 1, core_dev, core_in),
        (at_top, xhi == 0, xhi_dev, xhi_in),
    )

    @pl.when(z < last)
    def _():
        greet(above)

    greeted = 2 + jnp.where(z > 0, 1, 0)
    for member, earlier, peer, _ in pairs:
        pl.when(earlier & member)(functools.partial(greet, peer))
        greeted = greeted + jnp.where((~earlier) & member, 1, 0)
    for copy in loads:
        copy.start()
    pl.semaphore_wait(barrier, greeted)

    def tell(peer, sem):
        pl.semaphore_signal(sem, inc=1, device_id=peer, device_id_type=MESH)

    pl.when(z > 0)(functools.partial(tell, below, above_in))
    for member, earlier, peer, sem in pairs:
        pl.when((~earlier) & member)(functools.partial(tell, peer, sem))

    def know(pair):
        member, earlier, _, sem = pair
        pl.when(earlier & member)(lambda: pl.semaphore_wait(sem, 1))

    def wpiece(direction, j, extra):
        away = j // 2 + extra
        shard = (y + RING - away) % RING if direction == 0 else (y + away) % RING
        half = (j % 2) ^ direction
        return wall.at[pl.ds(pl.multiple_of(shard * SHARD + half * PIECE, 16), PIECE)]

    def ag_copy(direction, j):
        there = wpiece(direction, j, 0)
        half = (j % 2) ^ direction
        src = w.at[0, pl.ds(half * PIECE, PIECE)] if j < 2 else there
        return remote(src, there, ag_ss.at[direction, j], ag_rs.at[direction, j], ring[direction])

    def ag_arrive(j):
        for direction in (0, 1):
            here = wpiece(direction, j, 1)
            remote(
                here, here, ag_ss.at[direction, j], ag_rs.at[direction, j], ring[direction]
            ).wait_recv()
            if j + 2 < HOPS:
                ag_copy(direction, j + 2).start()

    for j in (0, 1):
        for direction in (0, 1):
            ag_copy(direction, j).start()

    x_c = remote(c2.at[pl.ds(0, ROWS)], c2.at[pl.ds(ROWS, ROWS)], x_ss.at[0], x_rs.at[0], partner)
    x_n = remote(nsend, n2.at[pl.ds(ROWS, ROWS)], x_ss.at[1], x_rs.at[1], partner)
    x_dn = remote(dn_s, dn_r, x_ss.at[2], x_rs.at[2], partner)
    x_k = remote(k_s, k_r, x_ss.at[3], x_rs.at[3], partner)
    x_g = remote(gsum, gx_r, x_ss.at[4], x_rs.at[4], partner)
    loads[3].wait()
    know(pairs[0])
    x_c.start()

    def small_ring(buf, at, ss, rs, devs):
        def slot(direction, hop):
            return buf.at[(at + RING - hop) % RING if direction == 0 else (at + hop) % RING]

        def send(direction, hop):
            return remote(
                slot(direction, hop), slot(direction, hop),
                ss.at[direction, hop], rs.at[direction, hop], devs[direction],
            )

        def arrive(hop):
            for direction in (0, 1):
                if hop < 4 - direction:
                    here = slot(direction, hop + 1)
                    remote(
                        here, here, ss.at[direction, hop], rs.at[direction, hop], devs[direction]
                    ).wait_recv()
                    if hop + 1 < 4 - direction:
                        send(direction, hop + 1).start()

        return send, arrive

    g_send, g_arrive = small_ring(gring, y, g_ss, g_rs, ring)

    z_up = remote(zacc, zin_r, z_ss.at[0], z_rs.at[0], above)
    z_core = remote(zacc, core_r, z_ss.at[1], z_rs.at[1], core_dev)
    z_xhi = remote(csum, xhi_r, z_ss.at[2], z_rs.at[2], xhi_dev)
    z_down = remote(ztotal, ztotal, z_ss.at[3], z_rs.at[3], below)

    def z_rise(low, high):
        @pl.when((z >= low) & (z <= high))
        def _():
            if low > 0:
                z_up.wait_recv()
                zacc[...] = zacc[...] + zin_r[...]
            if high < last:
                pl.semaphore_wait(above_in, 1)
                z_up.start()

        if high == last:

            know(pairs[1])
            know(pairs[2])

            @pl.when(z == last)
            def _():
                z_core.start()

    def z_turn_core():
        @pl.when(z == last)
        def _():
            z_core.wait_recv()
            csum[...] = zacc[...] + core_r[...]
            z_xhi.start()

    def z_turn_x():
        @pl.when(z == last)
        def _():
            z_xhi.wait_recv()
            ztotal[...] = csum[...] + xhi_r[...]
            z_down.start()

    def z_fall(at):
        @pl.when(z == at)
        def _():
            z_down.wait_recv()
            if at > 0:
                z_down.start()

    loads[0].wait()
    zacc[pl.ds(0, 4), :] = fragv[:, pl.ds(0, HALF)].astype(f32)
    zacc[pl.ds(4, 4), :] = fragv[:, pl.ds(HALF, HALF)].astype(f32)

    loads[1].wait()
    loads[2].wait()
    mine = x * HALF
    other = (1 - x) * HALF
    step = 768

    def cols(base, at):
        return pl.ds(pl.multiple_of(base + at, 128), step)

    def norm_block(i, _):
        rows = pl.ds(pl.multiple_of(i * 16, 16), 16)
        total = jnp.zeros((16, 128), f32)
        for at in range(0, D, step):
            v = tokv[rows, pl.ds(at, step)].astype(f32)
            v = v * v
            for k in range(0, step, 128):
                total = total + v[:, k : k + 128]
        mean = jnp.sum(total, axis=-1, keepdims=True) * (1.0 / D)
        rstd = lax.rsqrt(mean + eps)
        rstdv[rows, :] = jnp.broadcast_to(rstd, (16, 128))
        for base, to in ((other, nsend), (mine, n2)):
            for at in range(0, HALF, step):
                unit = tokv[rows, cols(base, at)].astype(f32) * rstd
                to[rows, pl.ds(at, step)] = (unit * (1.0 + gainv[:, cols(base, at)])).astype(bf16)
        return 0

    lax.fori_loop(0, ROWS // 16, norm_block, 0)
    x_n.start()
    z_rise(0, 0)

    ag_arrive(0)
    z_rise(1, 2)
    ag_arrive(1)
    z_rise(3, 4)
    ag_arrive(2)
    z_rise(5, 6)
    z_rise(7, 7)
    ag_arrive(3)
    z_turn_core()

    x_c.wait_recv()
    x_n.wait_recv()

    def part_block(i, _):
        at = pl.multiple_of(i * 256, 256)
        part[pl.ds(at, 256), :] = lax.dot_general(
            n2[:, pl.ds(at, 256)], c2[...], (((0,), (0,)), ((), ())), preferred_element_type=f32
        )
        return 0

    lax.fori_loop(0, HALF // 256, part_block, 0)

    ag_arrive(4)
    z_turn_x()

    def part_rows(direction, away, half, cut):
        shard = (y + away) % RING if direction == 0 else (y + RING - away) % RING
        return pl.ds(pl.multiple_of(shard * SHARD + half * PIECE + cut * CUT, 16), CUT)

    def rs_copy(direction, j, cut):
        rows = pl.ds(cut * CUT, CUT)
        return remote(
            rs_s.at[direction, j, rows], rs_r.at[direction, j, rows],
            rs_ss.at[direction, j, cut], rs_rs.at[direction, j, cut], ring[direction],
        )

    def rs_send(direction, j, cut):
        half, away = (j % 2) ^ direction, 4 - (j + 1) // 2
        rows = pl.ds(cut * CUT, CUT)
        v = part[part_rows(direction, away, half, cut), :]
        if j >= 2:
            v = v + rs_r[direction, j - 2, rows, :].astype(f32)
        rs_s[direction, j, rows, :] = v.astype(bf16)
        rs_copy(direction, j, cut).start()

    def rs_arrive(j):
        for cut in range(CUTS):
            for direction in (0, 1):
                rs_copy(direction, j, cut).wait_recv()
                rs_send(direction, j + 2, cut)

    for j in (0, 1):
        for cut in range(CUTS):
            for direction in (0, 1):
                rs_send(direction, j, cut)

    ag_arrive(5)
    z_fall(6)
    ag_arrive(6)
    z_fall(5)
    loads[4].wait()

    def dn_block(i, _):
        at = pl.multiple_of(i * 256, 256)
        v = lax.dot_general(
            c2[...], wall[pl.ds(at, 256), :], (((1,), (1,)), ((), ())), preferred_element_type=f32
        )
        dn_own[:, pl.ds(at, 256)] = v[:ROWS]
        dn_s[:, pl.ds(at, 256)] = v[ROWS:].astype(bf16)
        gring[y, :, pl.ds(at, 256)] = jnp.sum(
            v * n2[:, pl.ds(at, 256)].astype(f32), axis=0, keepdims=True
        )
        return 0

    lax.fori_loop(0, HALF // 256, dn_block, 0)
    x_dn.start()
    g_send(0, 0).start()
    g_send(1, 0).start()

    def key_block(i, _):
        at = pl.multiple_of(i * 256, 256)
        v = jnp.dot(n2[...], wall[:, pl.ds(at, 256)], preferred_element_type=f32)
        k_own[:, pl.ds(at, 256)] = v[:ROWS]
        k_s[:, pl.ds(at, 256)] = v[ROWS:].astype(bf16)
        return 0

    lax.fori_loop(0, KV // 256, key_block, 0)
    x_k.start()

    rs_arrive(0)
    z_fall(4)
    g_arrive(0)

    rs_arrive(1)
    z_fall(3)
    g_arrive(1)
    rs_arrive(2)
    z_fall(2)
    g_arrive(2)
    rs_arrive(3)
    z_fall(1)
    g_arrive(3)

    total = gring[0]
    for k in range(1, RING):
        total = total + gring[k]
    gsum[...] = total / (1.0 + gainv[:, pl.ds(pl.multiple_of(mine, 128), HALF)])
    x_g.start()

    x_k.wait_recv()

    def keys_block(i, _):
        rows = pl.ds(pl.multiple_of(i * 16, 16), 16)
        keys_o[rows, :] = (k_own[rows, :] + k_r[rows, :].astype(f32)).astype(bf16)
        return 0

    lax.fori_loop(0, ROWS // 16, keys_block, 0)

    x_dn.wait_recv()
    rs_arrive(4)
    z_fall(0)

    def gtok_block(i, _):
        rows = pl.ds(pl.multiple_of(i * 16, 16), 16)
        rstd = rstdv[rows, pl.ds(0, 1)]
        total = jnp.zeros((16, 128), f32)
        for base, grad in ((mine, dn_own), (other, dn_r)):
            for at in range(0, HALF, step):
                unit = tokv[rows, cols(base, at)].astype(f32) * rstd
                scaled = grad[rows, pl.ds(at, step)].astype(f32) * (1.0 + gainv[:, cols(base, at)])
                v = scaled * unit
                for k in range(0, step, 128):
                    total = total + v[:, k : k + 128]
        mean = jnp.sum(total, axis=-1, keepdims=True) * (1.0 / D)
        for base, grad in ((mine, dn_own), (other, dn_r)):
            for at in range(0, HALF, step):
                unit = tokv[rows, cols(base, at)].astype(f32) * rstd
                scaled = grad[rows, pl.ds(at, step)].astype(f32) * (1.0 + gainv[:, cols(base, at)])
                gtok_o[rows, cols(base, at)] = (rstd * (scaled - unit * mean)).astype(bf16)
        return 0

    lax.fori_loop(0, ROWS // 16, gtok_block, 0)

    loads[5].wait()
    loads[6].wait()
    for k in (0, 1):
        here = pl.ds(k * HALF, HALF)
        locals_sum = ztotal[pl.ds(4 * k, 4), :]
        g = globv[:, here]
        average = (32.0 * g - locals_sum) * (1.0 / 32.0)
        momentum = 0.9 * momv[:, here] + average
        nmom_o[:, here] = momentum
        nglob_o[:, here] = g - 0.7 * (average + 0.9 * momentum)

    x_g.wait_recv()
    ggain_o[:, pl.ds(pl.multiple_of(mine, 128), HALF)] = gsum[...]
    ggain_o[:, pl.ds(pl.multiple_of(other, 128), HALF)] = gx_r[...]

    for cut in range(CUTS):
        for direction in (0, 1):
            rs_copy(direction, 5, cut).wait_recv()
            rows = part_rows(0, 0, 1 - direction, cut)
            part[rows, :] = part[rows, :] + rs_r[direction, 5, pl.ds(cut * CUT, CUT), :].astype(f32)
    for cut in range(CUTS):
        for direction in (0, 1):
            rs_copy(direction, 6, cut).wait_recv()
            v = part[part_rows(0, 0, direction, cut), :]
            v = v + rs_r[direction, 6, pl.ds(cut * CUT, CUT), :].astype(f32)
            gw_o[0, pl.ds(direction * PIECE + cut * CUT, CUT), :] = v.astype(bf16)

    for direction in (0, 1):
        for j in range(HOPS):
            ag_copy(direction, j).wait_send()
            for cut in range(CUTS):
                rs_copy(direction, j, cut).wait_send()
        for hop in range(4 - direction):
            g_send(direction, hop).wait_send()
    for copy in (x_c, x_n, x_dn, x_k, x_g):
        copy.wait_send()

    @pl.when(z < last)
    def _():
        z_up.wait_send()

    @pl.when(z == last)
    def _():
        z_core.wait_send()
        z_xhi.wait_send()

    @pl.when(z > 0)
    def _():
        z_down.wait_send()


def hand_over(*refs):
    sources, results, sems = refs[:6], refs[6:12], refs[12]
    copies = [
        pltpu.make_async_copy(src, dst, sems.at[i])
        for i, (src, dst) in enumerate(zip(sources, results))
    ]
    for copy in copies:
        copy.start()
    for copy in copies:
        copy.wait()


def on_device(tokens, gain, key_weight, key_cotangent, local_fragment, global_fragment, outer_momentum):
    v, dma = pltpu.VMEM, pltpu.SemaphoreType.DMA
    hbm, anywhere = pl.BlockSpec(memory_space=pltpu.HBM), pl.BlockSpec(memory_space=pl.ANY)
    shapes = (
        jax.ShapeDtypeStruct((ROWS, KV), bf16),
        jax.ShapeDtypeStruct((ROWS, D), bf16),
        jax.ShapeDtypeStruct((1, SHARD, KV), bf16),
        jax.ShapeDtypeStruct((1, D), f32),
        jax.ShapeDtypeStruct((4, D), f32),
        jax.ShapeDtypeStruct((4, D), f32),
    )
    args = (tokens, gain, key_weight, key_cotangent, local_fragment, global_fragment, outer_momentum)
    args = [pltpu.with_memory_space_constraint(a, pltpu.HBM) for a in args]
    outs = pl.pallas_call(
        kernel,
        out_shape=[v(s.shape, s.dtype) for s in shapes],
        in_specs=[hbm] * 7,
        out_specs=[pl.BlockSpec(memory_space=pltpu.VMEM)] * 6,
        scratch_shapes=[
            v((ROWS, D), bf16),
            v((1, D), f32),
            v((2 * ROWS, HALF), bf16),
            v((ROWS, HALF), bf16),
            v((2 * ROWS, KV), bf16),
            v((HALF, KV), bf16),
            v((HALF, KV), f32),
            v((2, HOPS, PIECE, KV), bf16),
            v((2, HOPS, PIECE, KV), bf16),
            v((ROWS, HALF), f32),
            v((ROWS, HALF), bf16),
            v((ROWS, HALF), bf16),
            v((ROWS, KV), f32),
            v((ROWS, KV), bf16),
            v((ROWS, KV), bf16),
            v((ROWS, 128), f32),
            v((4, D), bf16),
            v((4, D), f32),
            v((4, D), f32),
            v((8, HALF), f32),
            v((8, HALF), f32),
            v((8, HALF), f32),
            v((8, HALF), f32),
            v((8, HALF), f32),
            v((8, HALF), f32),
            v((RING, 1, HALF), f32),
            v((1, HALF), f32),
            v((1, HALF), f32),
            dma((2, HOPS)),
            dma((2, HOPS)),
            dma((2, HOPS, CUTS)),
            dma((2, HOPS, CUTS)),
            dma((5,)),
            dma((5,)),
            dma((4,)),
            dma((4,)),
            dma((2, 4)),
            dma((2, 4)),
            pltpu.SemaphoreType.REGULAR,
            pltpu.SemaphoreType.REGULAR,
            pltpu.SemaphoreType.REGULAR,
            pltpu.SemaphoreType.REGULAR,
            dma((7,)),
        ],
        compiler_params=pltpu.CompilerParams(
            collective_id=0, has_side_effects=True, vmem_limit_bytes=48 * 2**20
        ),
        cost_estimate=pl.CostEstimate(
            flops=6 * ROWS * D * KV, bytes_accessed=8 * 2**20, transcendentals=ROWS
        ),
    )(*args)
    return pl.pallas_call(
        hand_over,
        out_shape=shapes,
        in_specs=[anywhere] * 6,
        out_specs=[hbm] * 6,
        scratch_shapes=[dma((6,))],
        compiler_params=pltpu.CompilerParams(vmem_limit_bytes=2**20),
    )(*[pltpu.with_memory_space_constraint(a, pltpu.VMEM) for a in outs])


def solution(mesh):
    placed = (
        P(("replica", "fsdp"), None),
        P("replica", None),
        P("replica", "fsdp", None),
        P(("replica", "fsdp"), None),
        P("replica", "fsdp", None),
        P("fsdp", None),
        P("fsdp", None),
    )
    return jax.shard_map(
        on_device,
        mesh=mesh,
        in_specs=placed,
        out_specs=(
            P(("replica", "fsdp"), None),
            P(("replica", "fsdp"), None),
            P("replica", "fsdp", None),
            P("replica", None),
            P("fsdp", None),
            P("fsdp", None),
        ),
        check_vma=False,
    )
```

```python
import functools

import jax
import jax.numpy as jnp
from jax import lax
from jax.experimental import pallas as pl
from jax.experimental.pallas import tpu as pltpu
from jax.sharding import PartitionSpec as P

eps = 1e-06
MESH = pl.DeviceIdType.MESH
f32, bf16 = jnp.float32, jnp.bfloat16

RING = 8
ROWS = 160
D = 4608
HALF = D // 2
KV = 1024
SHARD = 288
PIECE = SHARD // 2
HOPS = 7
CUTS = 1
CUT = PIECE // CUTS


def kernel(
    tok, gain, w, cot, frag, glob, mom,
    keys_o, gtok_o, gw_o, ggain_o, nglob_o, nmom_o,
    tokv, gainv, n2, nsend, c2, wall, part, rs_s, rs_r, dn_own, dn_s, dn_r, k_own, k_s, k_r,
    rstdv, fragv, globv, momv,
    nt, cn, pk_s, pk_r, zacc, zin_r, core_r, csum, xhi_r, ztotal, gring, gsum, gx_r,
    ag_ss, ag_rs, rs_ss, rs_rs, f_ss, f_rs, x_ss, x_rs, z_ss, z_rs, g_ss, g_rs, above_in, partner_in, core_in, xhi_in, loc,
):
    me = lax.axis_index("fsdp")
    rep = lax.axis_index("replica")
    x, y = me // RING, me % RING
    z, low = rep // 4, rep % 4
    core, xhi = low % 2, low // 2

    def fs(i):
        return {"fsdp": i}

    def rp(i):
        return {"replica": i}

    ring = (fs(x * RING + (y + 1) % RING), fs(x * RING + (y + RING - 1) % RING))
    last = RING - 1
    above, below = rp((z + 1) % RING * 4 + low), rp((z + last) % RING * 4 + low)
    partner = fs((1 - x) * RING + y)
    core_dev = rp(rep + 1 - 2 * core)
    xhi_dev = rp(rep + 2 - 4 * xhi)

    def local(i, src, dst):
        return pltpu.make_async_copy(src, dst, loc.at[i])

    def remote(src, dst, ss, rs, dev):
        return pltpu.make_async_remote_copy(
            src_ref=src, dst_ref=dst, send_sem=ss, recv_sem=rs, device_id=dev, device_id_type=MESH
        )

    own_rows = pl.ds(pl.multiple_of(y * SHARD, 16), SHARD)
    loads = [
        local(0, frag.at[0], fragv),
        local(1, tok, tokv),
        local(2, gain, gainv),
        local(3, cot, c2.at[pl.ds(0, ROWS)]),
        local(4, w.at[0], wall.at[own_rows]),
        local(5, glob, globv),
        local(6, mom, momv),
    ]

    barrier = pltpu.get_barrier_semaphore()

    def greet(peer):
        pl.semaphore_signal(barrier, inc=1, device_id=peer, device_id_type=MESH)

    for peer in ring:
        greet(peer)

    at_top = z == last
    pairs = (
        (True, x == 0, partner, partner_in),
        (at_top, core == 1, core_dev, core_in),
        (at_top, xhi == 0, xhi_dev, xhi_in),
    )

    @pl.when(z < last)
    def _():
        greet(above)

    greeted = 2 + jnp.where(z > 0, 1, 0)
    for member, earlier, peer, _ in pairs:
        pl.when(earlier & member)(functools.partial(greet, peer))
        greeted = greeted + jnp.where((~earlier) & member, 1, 0)
    for copy in loads:
        copy.start()
    pl.semaphore_wait(barrier, greeted)

    def tell(peer, sem):
        pl.semaphore_signal(sem, inc=1, device_id=peer, device_id_type=MESH)

    pl.when(z > 0)(functools.partial(tell, below, above_in))
    for member, earlier, peer, sem in pairs:
        pl.when((~earlier) & member)(functools.partial(tell, peer, sem))

    def know(pair):
        member, earlier, _, sem = pair
        pl.when(earlier & member)(lambda: pl.semaphore_wait(sem, 1))

    def wpiece(direction, j, extra):
        away = j // 2 + extra
        shard = (y + RING - away) % RING if direction == 0 else (y + away) % RING
        half = (j % 2) ^ direction
        return wall.at[pl.ds(pl.multiple_of(shard * SHARD + half * PIECE, 16), PIECE)]

    def ag_copy(direction, j):
        there = wpiece(direction, j, 0)
        half = (j % 2) ^ direction
        src = w.at[0, pl.ds(half * PIECE, PIECE)] if j < 2 else there
        return remote(src, there, ag_ss.at[direction, j], ag_rs.at[direction, j], ring[direction])

    def ag_arrive(j):
        for direction in (0, 1):
            here = wpiece(direction, j, 1)
            remote(
                here, here, ag_ss.at[direction, j], ag_rs.at[direction, j], ring[direction]
            ).wait_recv()
            if j + 2 < HOPS:
                ag_copy(direction, j + 2).start()

    for j in (0, 1):
        for direction in (0, 1):
            ag_copy(direction, j).start()

    x_c = remote(c2.at[pl.ds(0, ROWS)], c2.at[pl.ds(ROWS, ROWS)], x_ss.at[0], x_rs.at[0], partner)
    x_n = remote(nsend, n2.at[pl.ds(ROWS, ROWS)], x_ss.at[1], x_rs.at[1], partner)
    x_dn = remote(dn_s, dn_r, x_ss.at[2], x_rs.at[2], partner)
    x_k = remote(k_s, k_r, x_ss.at[3], x_rs.at[3], partner)
    x_g = remote(gsum, gx_r, x_ss.at[4], x_rs.at[4], partner)
    loads[3].wait()
    know(pairs[0])
    x_c.start()

    own, theirs = pl.ds(0, ROWS), pl.ds(ROWS, ROWS)

    def fc_copy(direction):
        return remote(
            c2.at[own], cn.at[direction, own],
            f_ss.at[0, direction], f_rs.at[0, direction], ring[direction],
        )

    def fx_copy(direction):
        return remote(
            cn.at[direction, own], cn.at[direction, theirs],
            f_ss.at[1, direction], f_rs.at[1, direction], partner,
        )

    def fn_copy(direction):
        return remote(
            pk_s.at[direction], pk_r.at[direction],
            f_ss.at[2, direction], f_rs.at[2, direction], ring[direction],
        )

    for direction in (0, 1):
        fc_copy(direction).start()

    def small_ring(buf, at, ss, rs, devs):
        def slot(direction, hop):
            return buf.at[(at + RING - hop) % RING if direction == 0 else (at + hop) % RING]

        def send(direction, hop):
            return remote(
                slot(direction, hop), slot(direction, hop),
                ss.at[direction, hop], rs.at[direction, hop], devs[direction],
            )

        def arrive(hop):
            for direction in (0, 1):
                if hop < 4 - direction:
                    here = slot(direction, hop + 1)
                    remote(
                        here, here, ss.at[direction, hop], rs.at[direction, hop], devs[direction]
                    ).wait_recv()
                    if hop + 1 < 4 - direction:
                        send(direction, hop + 1).start()

        return send, arrive

    g_send, g_arrive = small_ring(gring, y, g_ss, g_rs, ring)

    z_up = remote(zacc, zin_r, z_ss.at[0], z_rs.at[0], above)
    z_core = remote(zacc, core_r, z_ss.at[1], z_rs.at[1], core_dev)
    z_xhi = remote(csum, xhi_r, z_ss.at[2], z_rs.at[2], xhi_dev)
    z_down = remote(ztotal, ztotal, z_ss.at[3], z_rs.at[3], below)

    def z_rise(low, high):
        @pl.when((z >= low) & (z <= high))
        def _():
            if low > 0:
                z_up.wait_recv()
                zacc[...] = zacc[...] + zin_r[...]
            if high < last:
                pl.semaphore_wait(above_in, 1)
                z_up.start()

        if high == last:

            know(pairs[1])
            know(pairs[2])

            @pl.when(z == last)
            def _():
                z_core.start()

    def z_turn_core():
        @pl.when(z == last)
        def _():
            z_core.wait_recv()
            csum[...] = zacc[...] + core_r[...]
            z_xhi.start()

    def z_turn_x():
        @pl.when(z == last)
        def _():
            z_xhi.wait_recv()
            ztotal[...] = csum[...] + xhi_r[...]
            z_down.start()

    def z_fall(at):
        @pl.when(z == at)
        def _():
            z_down.wait_recv()
            if at > 0:
                z_down.start()

    loads[0].wait()
    zacc[pl.ds(0, 4), :] = fragv[:, pl.ds(0, HALF)].astype(f32)
    zacc[pl.ds(4, 4), :] = fragv[:, pl.ds(HALF, HALF)].astype(f32)

    loads[1].wait()
    loads[2].wait()
    mine = x * HALF
    other = (1 - x) * HALF
    step = 768

    def cols(base, at):
        return pl.ds(pl.multiple_of(base + at, 128), step)

    def norm_block(i, _):
        rows = pl.ds(pl.multiple_of(i * 16, 16), 16)
        total = jnp.zeros((16, 128), f32)
        for at in range(0, D, step):
            v = tokv[rows, pl.ds(at, step)].astype(f32)
            v = v * v
            for k in range(0, step, 128):
                total = total + v[:, k : k + 128]
        mean = jnp.sum(total, axis=-1, keepdims=True) * (1.0 / D)
        rstd = lax.rsqrt(mean + eps)
        rstdv[rows, :] = jnp.broadcast_to(rstd, (16, 128))
        for base, to in ((other, nsend), (mine, n2)):
            for at in range(0, HALF, step):
                unit = tokv[rows, cols(base, at)].astype(f32) * rstd
                to[rows, pl.ds(at, step)] = (unit * (1.0 + gainv[:, cols(base, at)])).astype(bf16)
        return 0

    lax.fori_loop(0, ROWS // 16, norm_block, 0)
    x_n.start()
    z_rise(0, 0)

    ag_arrive(0)
    z_rise(1, 2)
    ag_arrive(1)
    z_rise(3, 4)
    for direction in (0, 1):
        fc_copy(direction).wait_recv()
        fx_copy(direction).start()
    z_rise(5, 6)
    z_rise(7, 7)
    ag_arrive(2)
    z_turn_core()

    x_c.wait_recv()
    x_n.wait_recv()

    def part_block(i, _):
        at = pl.multiple_of(i * 256, 256)
        turned = n2[:, pl.ds(at, 256)].T
        nt[pl.ds(at, 256), :] = turned
        part[pl.ds(at, 256), :] = jnp.dot(turned, c2[...], preferred_element_type=f32)
        return 0

    lax.fori_loop(0, HALF // 256, part_block, 0)

    def part_rows(direction, away, half, cut):
        shard = (y + away) % RING if direction == 0 else (y + RING - away) % RING
        return pl.ds(pl.multiple_of(shard * SHARD + half * PIECE + cut * CUT, 16), CUT)

    def rs_copy(direction, j, cut):
        rows = pl.ds(cut * CUT, CUT)
        return remote(
            rs_s.at[direction, j, rows], rs_r.at[direction, j, rows],
            rs_ss.at[direction, j, cut], rs_rs.at[direction, j, cut], ring[direction],
        )

    def rs_send(direction, j, cut):
        half, away = (j % 2) ^ direction, 4 - (j + 1) // 2
        rows = pl.ds(cut * CUT, CUT)
        v = part[part_rows(direction, away, half, cut), :]
        if j >= 4:
            v = v + rs_r[direction, j - 2, rows, :].astype(f32)
        else:
            factor = (pk_r[direction, rows, pl.ds((j - 2) * 256, 256)], pk_r[direction, rows, pl.ds(512, 128)])
            zero = jnp.zeros((64, KV), bf16)
            rest = cn[direction, pl.ds(256, 64), :]
            rest = jnp.concatenate([rest, zero] if j == 2 else [zero, rest], axis=0)
            v = v + jnp.dot(factor[0], cn[direction, pl.ds(0, 256), :], preferred_element_type=f32)
            v = v + jnp.dot(factor[1], rest, preferred_element_type=f32)
        rs_s[direction, j, rows, :] = v.astype(bf16)
        rs_copy(direction, j, cut).start()

    def rs_arrive(j):
        for direction in (0, 1):
            rs_copy(direction, j, 0).wait_recv()
        g_arrive(j - 2)
        for direction in (0, 1):
            rs_send(direction, j + 2, 0)

    def pack(direction):
        a, b = (nt[part_rows(direction, 4 - j, (j % 2) ^ direction, 0), :] for j in (0, 1))
        pk_s[direction, :, :] = jnp.concatenate(
            [a[:, :256], b[:, :256], a[:, 256:], b[:, 256:]], axis=1
        )
        fn_copy(direction).start()

    for direction in (0, 1):
        pack(direction)

    ag_arrive(3)
    z_turn_x()

    ag_arrive(4)
    z_fall(6)

    for direction in (0, 1):
        fn_copy(direction).wait_recv()
        fx_copy(direction).wait_recv()
        rs_send(direction, 2, 0)

    ag_arrive(5)
    z_fall(5)
    ag_arrive(6)
    z_fall(4)
    loads[4].wait()

    def dn_block(i, _):
        at = pl.multiple_of(i * 256, 256)
        v = lax.dot_general(
            c2[...], wall[pl.ds(at, 256), :], (((1,), (1,)), ((), ())), preferred_element_type=f32
        )
        dn_own[:, pl.ds(at, 256)] = v[:ROWS]
        dn_s[:, pl.ds(at, 256)] = v[ROWS:].astype(bf16)
        gring[y, :, pl.ds(at, 256)] = jnp.sum(
            v * n2[:, pl.ds(at, 256)].astype(f32), axis=0, keepdims=True
        )
        return 0

    lax.fori_loop(0, HALF // 256, dn_block, 0)
    x_dn.start()
    g_send(0, 0).start()
    g_send(1, 0).start()
    rs_send(0, 3, 0)
    rs_send(1, 3, 0)

    def key_block(i, _):
        at = pl.multiple_of(i * 256, 256)
        v = jnp.dot(n2[...], wall[:, pl.ds(at, 256)], preferred_element_type=f32)
        k_own[:, pl.ds(at, 256)] = v[:ROWS]
        k_s[:, pl.ds(at, 256)] = v[ROWS:].astype(bf16)
        return 0

    lax.fori_loop(0, KV // 256, key_block, 0)
    x_k.start()

    rs_arrive(2)
    z_fall(3)
    rs_arrive(3)
    z_fall(2)
    rs_arrive(4)
    z_fall(1)

    x_dn.wait_recv()

    def gtok_block(i, _):
        rows = pl.ds(pl.multiple_of(i * 16, 16), 16)
        rstd = rstdv[rows, pl.ds(0, 1)]
        total = jnp.zeros((16, 128), f32)
        for base, grad in ((mine, dn_own), (other, dn_r)):
            for at in range(0, HALF, step):
                unit = tokv[rows, cols(base, at)].astype(f32) * rstd
                scaled = grad[rows, pl.ds(at, step)].astype(f32) * (1.0 + gainv[:, cols(base, at)])
                v = scaled * unit
                for k in range(0, step, 128):
                    total = total + v[:, k : k + 128]
        mean = jnp.sum(total, axis=-1, keepdims=True) * (1.0 / D)
        for base, grad in ((mine, dn_own), (other, dn_r)):
            for at in range(0, HALF, step):
                unit = tokv[rows, cols(base, at)].astype(f32) * rstd
                scaled = grad[rows, pl.ds(at, step)].astype(f32) * (1.0 + gainv[:, cols(base, at)])
                gtok_o[rows, cols(base, at)] = (rstd * (scaled - unit * mean)).astype(bf16)
        return 0

    lax.fori_loop(0, ROWS // 16, gtok_block, 0)

    for cut in range(CUTS):
        for direction in (0, 1):
            rs_copy(direction, 5, cut).wait_recv()
            rows = part_rows(0, 0, 1 - direction, cut)
            part[rows, :] = part[rows, :] + rs_r[direction, 5, pl.ds(cut * CUT, CUT), :].astype(f32)
    z_fall(0)
    g_arrive(3)

    total = gring[0]
    for k in range(1, RING):
        total = total + gring[k]
    gsum[...] = total / (1.0 + gainv[:, pl.ds(pl.multiple_of(mine, 128), HALF)])
    x_g.start()

    loads[5].wait()
    loads[6].wait()
    for k in (0, 1):
        here = pl.ds(k * HALF, HALF)
        locals_sum = ztotal[pl.ds(4 * k, 4), :]
        g = globv[:, here]
        average = (32.0 * g - locals_sum) * (1.0 / 32.0)
        momentum = 0.9 * momv[:, here] + average
        nmom_o[:, here] = momentum
        nglob_o[:, here] = g - 0.7 * (average + 0.9 * momentum)

    x_k.wait_recv()

    def keys_block(i, _):
        rows = pl.ds(pl.multiple_of(i * 16, 16), 16)
        keys_o[rows, :] = (k_own[rows, :] + k_r[rows, :].astype(f32)).astype(bf16)
        return 0

    lax.fori_loop(0, ROWS // 16, keys_block, 0)

    for cut in range(CUTS):
        for direction in (0, 1):
            rs_copy(direction, 6, cut).wait_recv()
            v = part[part_rows(0, 0, direction, cut), :]
            v = v + rs_r[direction, 6, pl.ds(cut * CUT, CUT), :].astype(f32)
            gw_o[0, pl.ds(direction * PIECE + cut * CUT, CUT), :] = v.astype(bf16)

    x_g.wait_recv()
    ggain_o[:, pl.ds(pl.multiple_of(mine, 128), HALF)] = gsum[...]
    ggain_o[:, pl.ds(pl.multiple_of(other, 128), HALF)] = gx_r[...]

    for direction in (0, 1):
        for j in range(HOPS):
            ag_copy(direction, j).wait_send()
            if j >= 2:
                for cut in range(CUTS):
                    rs_copy(direction, j, cut).wait_send()
        for copy in (fc_copy, fx_copy, fn_copy):
            copy(direction).wait_send()
        for hop in range(4 - direction):
            g_send(direction, hop).wait_send()
    for copy in (x_c, x_n, x_dn, x_k, x_g):
        copy.wait_send()

    @pl.when(z < last)
    def _():
        z_up.wait_send()

    @pl.when(z == last)
    def _():
        z_core.wait_send()
        z_xhi.wait_send()

    @pl.when(z > 0)
    def _():
        z_down.wait_send()


def hand_over(*refs):
    sources, results, sems = refs[:6], refs[6:12], refs[12]
    copies = [
        pltpu.make_async_copy(src, dst, sems.at[i])
        for i, (src, dst) in enumerate(zip(sources, results))
    ]
    for copy in copies:
        copy.start()
    for copy in copies:
        copy.wait()


def on_device(tokens, gain, key_weight, key_cotangent, local_fragment, global_fragment, outer_momentum):
    v, dma = pltpu.VMEM, pltpu.SemaphoreType.DMA
    hbm, anywhere = pl.BlockSpec(memory_space=pltpu.HBM), pl.BlockSpec(memory_space=pl.ANY)
    shapes = (
        jax.ShapeDtypeStruct((ROWS, KV), bf16),
        jax.ShapeDtypeStruct((ROWS, D), bf16),
        jax.ShapeDtypeStruct((1, SHARD, KV), bf16),
        jax.ShapeDtypeStruct((1, D), f32),
        jax.ShapeDtypeStruct((4, D), f32),
        jax.ShapeDtypeStruct((4, D), f32),
    )
    args = (tokens, gain, key_weight, key_cotangent, local_fragment, global_fragment, outer_momentum)
    args = [pltpu.with_memory_space_constraint(a, pltpu.HBM) for a in args]
    outs = pl.pallas_call(
        kernel,
        out_shape=[v(s.shape, s.dtype) for s in shapes],
        in_specs=[hbm] * 7,
        out_specs=[pl.BlockSpec(memory_space=pltpu.VMEM)] * 6,
        scratch_shapes=[
            v((ROWS, D), bf16),
            v((1, D), f32),
            v((2 * ROWS, HALF), bf16),
            v((ROWS, HALF), bf16),
            v((2 * ROWS, KV), bf16),
            v((HALF, KV), bf16),
            v((HALF, KV), f32),
            v((2, HOPS, PIECE, KV), bf16),
            v((2, HOPS, PIECE, KV), bf16),
            v((ROWS, HALF), f32),
            v((ROWS, HALF), bf16),
            v((ROWS, HALF), bf16),
            v((ROWS, KV), f32),
            v((ROWS, KV), bf16),
            v((ROWS, KV), bf16),
            v((ROWS, 128), f32),
            v((4, D), bf16),
            v((4, D), f32),
            v((4, D), f32),
            v((HALF, 2 * ROWS), bf16),
            v((2, 2 * ROWS, KV), bf16),
            v((2, PIECE, 4 * ROWS), bf16),
            v((2, PIECE, 4 * ROWS), bf16),
            v((8, HALF), f32),
            v((8, HALF), f32),
            v((8, HALF), f32),
            v((8, HALF), f32),
            v((8, HALF), f32),
            v((8, HALF), f32),
            v((RING, 1, HALF), f32),
            v((1, HALF), f32),
            v((1, HALF), f32),
            dma((2, HOPS)),
            dma((2, HOPS)),
            dma((2, HOPS, CUTS)),
            dma((2, HOPS, CUTS)),
            dma((3, 2)),
            dma((3, 2)),
            dma((5,)),
            dma((5,)),
            dma((4,)),
            dma((4,)),
            dma((2, 4)),
            dma((2, 4)),
            pltpu.SemaphoreType.REGULAR,
            pltpu.SemaphoreType.REGULAR,
            pltpu.SemaphoreType.REGULAR,
            pltpu.SemaphoreType.REGULAR,
            dma((7,)),
        ],
        compiler_params=pltpu.CompilerParams(
            collective_id=0, has_side_effects=True, vmem_limit_bytes=48 * 2**20
        ),
        cost_estimate=pl.CostEstimate(
            flops=6 * ROWS * D * KV, bytes_accessed=8 * 2**20, transcendentals=ROWS
        ),
    )(*args)
    return pl.pallas_call(
        hand_over,
        out_shape=shapes,
        in_specs=[anywhere] * 6,
        out_specs=[hbm] * 6,
        scratch_shapes=[dma((6,))],
        compiler_params=pltpu.CompilerParams(vmem_limit_bytes=2**20),
    )(*[pltpu.with_memory_space_constraint(a, pltpu.VMEM) for a in outs])


def solution(mesh):
    placed = (
        P(("replica", "fsdp"), None),
        P("replica", None),
        P("replica", "fsdp", None),
        P(("replica", "fsdp"), None),
        P("replica", "fsdp", None),
        P("fsdp", None),
        P("fsdp", None),
    )
    return jax.shard_map(
        on_device,
        mesh=mesh,
        in_specs=placed,
        out_specs=(
            P(("replica", "fsdp"), None),
            P(("replica", "fsdp"), None),
            P("replica", "fsdp", None),
            P("replica", None),
            P("fsdp", None),
            P("fsdp", None),
        ),
        check_vma=False,
    )
```

```python
import functools

import jax
import jax.numpy as jnp
from jax import lax
from jax.experimental import pallas as pl
from jax.experimental.pallas import tpu as pltpu
from jax.sharding import PartitionSpec as P

eps = 1e-06
MESH = pl.DeviceIdType.MESH
f32, bf16 = jnp.float32, jnp.bfloat16

RING = 8
ROWS = 160
D = 4608
HALF = D // 2
KV = 1024
SHARD = 288
PIECE = SHARD // 2
HOPS = 7
CUTS = 1
CUT = PIECE // CUTS


def kernel(
    tok, gain, w, cot, frag, glob, mom,
    keys_o, gtok_o, gw_o, ggain_o, nglob_o, nmom_o,
    tokv, gainv, n2, nsend, c2, wall, part, rs_s, rs_r, dn_own, dn_s, dn_r, k_own, k_s, k_r,
    rstdv, fragv, globv, momv,
    nt, cn, pk_s, pk_r, zacc, zin_r, core_r, csum, xhi_r, ztotal, gring, gsum, gx_r,
    ag_ss, ag_rs, rs_ss, rs_rs, f_ss, f_rs, x_ss, x_rs, z_ss, z_rs, g_ss, g_rs, above_in, partner_in, core_in, xhi_in, loc,
):
    me = lax.axis_index("fsdp")
    rep = lax.axis_index("replica")
    x, y = me // RING, me % RING
    z, low = rep // 4, rep % 4
    core, xhi = low % 2, low // 2

    def fs(i):
        return {"fsdp": i}

    def rp(i):
        return {"replica": i}

    ring = (fs(x * RING + (y + 1) % RING), fs(x * RING + (y + RING - 1) % RING))
    last = RING - 1
    above, below = rp((z + 1) % RING * 4 + low), rp((z + last) % RING * 4 + low)
    partner = fs((1 - x) * RING + y)
    core_dev = rp(rep + 1 - 2 * core)
    xhi_dev = rp(rep + 2 - 4 * xhi)

    def local(i, src, dst):
        return pltpu.make_async_copy(src, dst, loc.at[i])

    def remote(src, dst, ss, rs, dev):
        return pltpu.make_async_remote_copy(
            src_ref=src, dst_ref=dst, send_sem=ss, recv_sem=rs, device_id=dev, device_id_type=MESH
        )

    own_rows = pl.ds(pl.multiple_of(y * SHARD, 16), SHARD)
    loads = [
        local(0, frag.at[0], fragv),
        local(1, tok, tokv),
        local(2, gain, gainv),
        local(3, cot, c2.at[pl.ds(0, ROWS)]),
        local(4, w.at[0], wall.at[own_rows]),
        local(5, glob, globv),
        local(6, mom, momv),
    ]

    barrier = pltpu.get_barrier_semaphore()

    def greet(peer):
        pl.semaphore_signal(barrier, inc=1, device_id=peer, device_id_type=MESH)

    for peer in ring:
        greet(peer)

    at_top = z == last
    pairs = (
        (True, x == 0, partner, partner_in),
        (at_top, core == 1, core_dev, core_in),
        (at_top, xhi == 0, xhi_dev, xhi_in),
    )

    @pl.when(z < last)
    def _():
        greet(above)

    greeted = 2 + jnp.where(z > 0, 1, 0)
    for member, earlier, peer, _ in pairs:
        pl.when(earlier & member)(functools.partial(greet, peer))
        greeted = greeted + jnp.where((~earlier) & member, 1, 0)
    for copy in loads:
        copy.start()
    pl.semaphore_wait(barrier, greeted)

    def tell(peer, sem):
        pl.semaphore_signal(sem, inc=1, device_id=peer, device_id_type=MESH)

    pl.when(z > 0)(functools.partial(tell, below, above_in))
    for member, earlier, peer, sem in pairs:
        pl.when((~earlier) & member)(functools.partial(tell, peer, sem))

    def know(pair):
        member, earlier, _, sem = pair
        pl.when(earlier & member)(lambda: pl.semaphore_wait(sem, 1))

    def wpiece(direction, j, extra):
        away = j // 2 + extra
        shard = (y + RING - away) % RING if direction == 0 else (y + away) % RING
        half = (j % 2) ^ direction
        return wall.at[pl.ds(pl.multiple_of(shard * SHARD + half * PIECE, 16), PIECE)]

    def ag_copy(direction, j):
        there = wpiece(direction, j, 0)
        half = (j % 2) ^ direction
        src = w.at[0, pl.ds(half * PIECE, PIECE)] if j < 2 else there
        return remote(src, there, ag_ss.at[direction, j % 2], ag_rs.at[direction, j], ring[direction])

    def ag_arrive(j):
        for direction in (0, 1):
            here = wpiece(direction, j, 1)
            remote(
                here, here, ag_ss.at[direction, j % 2], ag_rs.at[direction, j], ring[direction]
            ).wait_recv()
            if j + 2 < HOPS:
                ag_copy(direction, j).wait_send()
                ag_copy(direction, j + 2).start()

    for j in (0, 1):
        for direction in (0, 1):
            ag_copy(direction, j).start()

    x_c = remote(c2.at[pl.ds(0, ROWS)], c2.at[pl.ds(ROWS, ROWS)], x_ss.at[0], x_rs.at[0], partner)
    x_n = remote(nsend, n2.at[pl.ds(ROWS, ROWS)], x_ss.at[1], x_rs.at[1], partner)
    x_dn = remote(dn_s, dn_r, x_ss.at[2], x_rs.at[2], partner)
    x_k = remote(k_s, k_r, x_ss.at[3], x_rs.at[3], partner)
    x_g = remote(gsum, gx_r, x_ss.at[4], x_rs.at[4], partner)
    loads[3].wait()
    know(pairs[0])
    x_c.start()

    own, theirs = pl.ds(0, ROWS), pl.ds(ROWS, ROWS)

    def fc_copy(direction):
        return remote(
            c2.at[own], cn.at[direction, own],
            f_ss.at[0, direction], f_rs.at[0, direction], ring[direction],
        )

    def fx_copy(direction):
        return remote(
            cn.at[direction, own], cn.at[direction, theirs],
            f_ss.at[1, direction], f_rs.at[1, direction], partner,
        )

    def fn_copy(direction):
        return remote(
            pk_s.at[direction], pk_r.at[direction],
            f_ss.at[2, direction], f_rs.at[2, direction], ring[direction],
        )

    for direction in (0, 1):
        fc_copy(direction).start()

    def small_ring(buf, at, ss, rs, devs):
        def slot(direction, hop):
            return buf.at[(at + RING - hop) % RING if direction == 0 else (at + hop) % RING]

        def send(direction, hop):
            return remote(
                slot(direction, hop), slot(direction, hop),
                ss.at[direction], rs.at[direction, hop], devs[direction],
            )

        def arrive(hop):
            for direction in (0, 1):
                if hop < 4 - direction:
                    here = slot(direction, hop + 1)
                    remote(
                        here, here, ss.at[direction], rs.at[direction, hop], devs[direction]
                    ).wait_recv()
                    if hop + 1 < 4 - direction:
                        send(direction, hop).wait_send()
                        send(direction, hop + 1).start()

        return send, arrive

    g_send, g_arrive = small_ring(gring, y, g_ss, g_rs, ring)

    z_up = remote(zacc, zin_r, z_ss.at[0], z_rs.at[0], above)
    z_core = remote(zacc, core_r, z_ss.at[1], z_rs.at[1], core_dev)
    z_xhi = remote(csum, xhi_r, z_ss.at[2], z_rs.at[2], xhi_dev)
    z_down = remote(ztotal, ztotal, z_ss.at[3], z_rs.at[3], below)

    def z_rise(low, high):
        @pl.when((z >= low) & (z <= high))
        def _():
            if low > 0:
                z_up.wait_recv()
                zacc[...] = zacc[...] + zin_r[...]
            if high < last:
                pl.semaphore_wait(above_in, 1)
                z_up.start()

        if high == last:

            know(pairs[1])
            know(pairs[2])

            @pl.when(z == last)
            def _():
                z_core.start()

    def z_turn_core():
        @pl.when(z == last)
        def _():
            z_core.wait_recv()
            csum[...] = zacc[...] + core_r[...]
            z_xhi.start()

    def z_turn_x():
        @pl.when(z == last)
        def _():
            z_xhi.wait_recv()
            ztotal[...] = csum[...] + xhi_r[...]
            z_down.start()

    def z_fall(at):
        @pl.when(z == at)
        def _():
            z_down.wait_recv()
            if at > 0:
                z_down.start()

    loads[0].wait()
    zacc[pl.ds(0, 4), :] = fragv[:, pl.ds(0, HALF)].astype(f32)
    zacc[pl.ds(4, 4), :] = fragv[:, pl.ds(HALF, HALF)].astype(f32)

    loads[1].wait()
    loads[2].wait()
    mine = x * HALF
    other = (1 - x) * HALF
    step = 768

    def cols(base, at):
        return pl.ds(pl.multiple_of(base + at, 128), step)

    def norm_block(i, _):
        rows = pl.ds(pl.multiple_of(i * 16, 16), 16)
        total = jnp.zeros((16, 128), f32)
        for at in range(0, D, step):
            v = tokv[rows, pl.ds(at, step)].astype(f32)
            v = v * v
            for k in range(0, step, 128):
                total = total + v[:, k : k + 128]
        mean = jnp.sum(total, axis=-1, keepdims=True) * (1.0 / D)
        rstd = lax.rsqrt(mean + eps)
        rstdv[rows, :] = jnp.broadcast_to(rstd, (16, 128))
        for base, to in ((other, nsend), (mine, n2)):
            for at in range(0, HALF, step):
                unit = tokv[rows, cols(base, at)].astype(f32) * rstd
                to[rows, pl.ds(at, step)] = (unit * (1.0 + gainv[:, cols(base, at)])).astype(bf16)
        return 0

    lax.fori_loop(0, ROWS // 16, norm_block, 0)
    x_n.start()
    z_rise(0, 0)

    ag_arrive(0)
    z_rise(1, 2)
    ag_arrive(1)
    z_rise(3, 4)
    for direction in (0, 1):
        fc_copy(direction).wait_recv()
        fx_copy(direction).start()
    z_rise(5, 6)
    z_rise(7, 7)
    ag_arrive(2)
    z_turn_core()

    x_c.wait_recv()
    x_n.wait_recv()

    def part_block(i, _):
        at = pl.multiple_of(i * 256, 256)
        turned = n2[:, pl.ds(at, 256)].T
        nt[pl.ds(at, 256), :] = turned
        part[pl.ds(at, 256), :] = jnp.dot(turned, c2[...], preferred_element_type=f32)
        return 0

    lax.fori_loop(0, HALF // 256, part_block, 0)

    def part_rows(direction, away, half, cut):
        shard = (y + away) % RING if direction == 0 else (y + RING - away) % RING
        return pl.ds(pl.multiple_of(shard * SHARD + half * PIECE + cut * CUT, 16), CUT)

    def rs_copy(direction, j, cut):
        rows = pl.ds(cut * CUT, CUT)
        return remote(
            rs_s.at[direction, j, rows], rs_r.at[direction, j, rows],
            rs_ss.at[direction, j % 2, cut], rs_rs.at[direction, j - 2, cut], ring[direction],
        )

    def rs_send(direction, j, cut):
        half, away = (j % 2) ^ direction, 4 - (j + 1) // 2
        rows = pl.ds(cut * CUT, CUT)
        v = part[part_rows(direction, away, half, cut), :]
        if j >= 4:
            v = v + rs_r[direction, j - 2, rows, :].astype(f32)
        else:
            factor = (pk_r[direction, rows, pl.ds((j - 2) * 256, 256)], pk_r[direction, rows, pl.ds(512, 128)])
            zero = jnp.zeros((64, KV), bf16)
            rest = cn[direction, pl.ds(256, 64), :]
            rest = jnp.concatenate([rest, zero] if j == 2 else [zero, rest], axis=0)
            v = v + jnp.dot(factor[0], cn[direction, pl.ds(0, 256), :], preferred_element_type=f32)
            v = v + jnp.dot(factor[1], rest, preferred_element_type=f32)
        rs_s[direction, j, rows, :] = v.astype(bf16)
        if j >= 4:
            rs_copy(direction, j - 2, cut).wait_send()
        rs_copy(direction, j, cut).start()

    def rs_arrive(j):
        for direction in (0, 1):
            rs_copy(direction, j, 0).wait_recv()
        g_arrive(j - 2)
        for direction in (0, 1):
            rs_send(direction, j + 2, 0)

    def pack(direction):
        a, b = (nt[part_rows(direction, 4 - j, (j % 2) ^ direction, 0), :] for j in (0, 1))
        pk_s[direction, :, :] = jnp.concatenate(
            [a[:, :256], b[:, :256], a[:, 256:], b[:, 256:]], axis=1
        )
        fn_copy(direction).start()

    for direction in (0, 1):
        pack(direction)

    ag_arrive(3)
    z_turn_x()

    ag_arrive(4)
    z_fall(6)

    for direction in (0, 1):
        fn_copy(direction).wait_recv()
        fx_copy(direction).wait_recv()
        rs_send(direction, 2, 0)

    ag_arrive(5)
    z_fall(5)
    ag_arrive(6)
    z_fall(4)
    loads[4].wait()

    def dn_block(i, _):
        at = pl.multiple_of(i * 256, 256)
        v = lax.dot_general(
            c2[...], wall[pl.ds(at, 256), :], (((1,), (1,)), ((), ())), preferred_element_type=f32
        )
        dn_own[:, pl.ds(at, 256)] = v[:ROWS]
        dn_s[:, pl.ds(at, 256)] = v[ROWS:].astype(bf16)
        gring[y, :, pl.ds(at, 256)] = jnp.sum(
            v * n2[:, pl.ds(at, 256)].astype(f32), axis=0, keepdims=True
        )
        return 0

    lax.fori_loop(0, HALF // 256, dn_block, 0)
    x_dn.start()
    g_send(0, 0).start()
    g_send(1, 0).start()
    rs_send(0, 3, 0)
    rs_send(1, 3, 0)

    def key_block(i, _):
        at = pl.multiple_of(i * 256, 256)
        v = jnp.dot(n2[...], wall[:, pl.ds(at, 256)], preferred_element_type=f32)
        k_own[:, pl.ds(at, 256)] = v[:ROWS]
        k_s[:, pl.ds(at, 256)] = v[ROWS:].astype(bf16)
        return 0

    lax.fori_loop(0, KV // 256, key_block, 0)
    x_k.start()

    rs_arrive(2)
    z_fall(3)
    rs_arrive(3)
    z_fall(2)
    rs_arrive(4)
    z_fall(1)

    x_dn.wait_recv()

    def gtok_block(i, _):
        rows = pl.ds(pl.multiple_of(i * 16, 16), 16)
        rstd = rstdv[rows, pl.ds(0, 1)]
        total = jnp.zeros((16, 128), f32)
        for base, grad in ((mine, dn_own), (other, dn_r)):
            for at in range(0, HALF, step):
                unit = tokv[rows, cols(base, at)].astype(f32) * rstd
                scaled = grad[rows, pl.ds(at, step)].astype(f32) * (1.0 + gainv[:, cols(base, at)])
                v = scaled * unit
                for k in range(0, step, 128):
                    total = total + v[:, k : k + 128]
        mean = jnp.sum(total, axis=-1, keepdims=True) * (1.0 / D)
        for base, grad in ((mine, dn_own), (other, dn_r)):
            for at in range(0, HALF, step):
                unit = tokv[rows, cols(base, at)].astype(f32) * rstd
                scaled = grad[rows, pl.ds(at, step)].astype(f32) * (1.0 + gainv[:, cols(base, at)])
                gtok_o[rows, cols(base, at)] = (rstd * (scaled - unit * mean)).astype(bf16)
        return 0

    lax.fori_loop(0, ROWS // 16, gtok_block, 0)

    for cut in range(CUTS):
        for direction in (0, 1):
            rs_copy(direction, 5, cut).wait_recv()
            rows = part_rows(0, 0, 1 - direction, cut)
            part[rows, :] = part[rows, :] + rs_r[direction, 5, pl.ds(cut * CUT, CUT), :].astype(f32)
    z_fall(0)
    g_arrive(3)

    total = gring[0]
    for k in range(1, RING):
        total = total + gring[k]
    gsum[...] = total / (1.0 + gainv[:, pl.ds(pl.multiple_of(mine, 128), HALF)])
    x_g.start()

    loads[5].wait()
    loads[6].wait()
    for k in (0, 1):
        here = pl.ds(k * HALF, HALF)
        locals_sum = ztotal[pl.ds(4 * k, 4), :]
        g = globv[:, here]
        average = (32.0 * g - locals_sum) * (1.0 / 32.0)
        momentum = 0.9 * momv[:, here] + average
        nmom_o[:, here] = momentum
        nglob_o[:, here] = g - 0.7 * (average + 0.9 * momentum)

    x_k.wait_recv()

    def keys_block(i, _):
        rows = pl.ds(pl.multiple_of(i * 16, 16), 16)
        keys_o[rows, :] = (k_own[rows, :] + k_r[rows, :].astype(f32)).astype(bf16)
        return 0

    lax.fori_loop(0, ROWS // 16, keys_block, 0)

    for cut in range(CUTS):
        for direction in (0, 1):
            rs_copy(direction, 6, cut).wait_recv()
            v = part[part_rows(0, 0, direction, cut), :]
            v = v + rs_r[direction, 6, pl.ds(cut * CUT, CUT), :].astype(f32)
            gw_o[0, pl.ds(direction * PIECE + cut * CUT, CUT), :] = v.astype(bf16)

    x_g.wait_recv()
    ggain_o[:, pl.ds(pl.multiple_of(mine, 128), HALF)] = gsum[...]
    ggain_o[:, pl.ds(pl.multiple_of(other, 128), HALF)] = gx_r[...]

    for direction in (0, 1):
        for j in (HOPS - 2, HOPS - 1):
            ag_copy(direction, j).wait_send()
            for cut in range(CUTS):
                rs_copy(direction, j, cut).wait_send()
        for copy in (fc_copy, fx_copy, fn_copy):
            copy(direction).wait_send()
        g_send(direction, 3 - direction).wait_send()
    for copy in (x_c, x_n, x_dn, x_k, x_g):
        copy.wait_send()

    @pl.when(z < last)
    def _():
        z_up.wait_send()

    @pl.when(z == last)
    def _():
        z_core.wait_send()
        z_xhi.wait_send()

    @pl.when(z > 0)
    def _():
        z_down.wait_send()


def hand_over(*refs):
    sources, results, sems = refs[:6], refs[6:12], refs[12]
    copies = [
        pltpu.make_async_copy(src, dst, sems.at[i])
        for i, (src, dst) in enumerate(zip(sources, results))
    ]
    for copy in copies:
        copy.start()
    for copy in copies:
        copy.wait()


def on_device(tokens, gain, key_weight, key_cotangent, local_fragment, global_fragment, outer_momentum):
    v, dma = pltpu.VMEM, pltpu.SemaphoreType.DMA
    hbm, anywhere = pl.BlockSpec(memory_space=pltpu.HBM), pl.BlockSpec(memory_space=pl.ANY)
    shapes = (
        jax.ShapeDtypeStruct((ROWS, KV), bf16),
        jax.ShapeDtypeStruct((ROWS, D), bf16),
        jax.ShapeDtypeStruct((1, SHARD, KV), bf16),
        jax.ShapeDtypeStruct((1, D), f32),
        jax.ShapeDtypeStruct((4, D), f32),
        jax.ShapeDtypeStruct((4, D), f32),
    )
    args = (tokens, gain, key_weight, key_cotangent, local_fragment, global_fragment, outer_momentum)
    args = [pltpu.with_memory_space_constraint(a, pltpu.HBM) for a in args]
    outs = pl.pallas_call(
        kernel,
        out_shape=[v(s.shape, s.dtype) for s in shapes],
        in_specs=[hbm] * 7,
        out_specs=[pl.BlockSpec(memory_space=pltpu.VMEM)] * 6,
        scratch_shapes=[
            v((ROWS, D), bf16),
            v((1, D), f32),
            v((2 * ROWS, HALF), bf16),
            v((ROWS, HALF), bf16),
            v((2 * ROWS, KV), bf16),
            v((HALF, KV), bf16),
            v((HALF, KV), f32),
            v((2, HOPS, PIECE, KV), bf16),
            v((2, HOPS, PIECE, KV), bf16),
            v((ROWS, HALF), f32),
            v((ROWS, HALF), bf16),
            v((ROWS, HALF), bf16),
            v((ROWS, KV), f32),
            v((ROWS, KV), bf16),
            v((ROWS, KV), bf16),
            v((ROWS, 128), f32),
            v((4, D), bf16),
            v((4, D), f32),
            v((4, D), f32),
            v((HALF, 2 * ROWS), bf16),
            v((2, 2 * ROWS, KV), bf16),
            v((2, PIECE, 4 * ROWS), bf16),
            v((2, PIECE, 4 * ROWS), bf16),
            v((8, HALF), f32),
            v((8, HALF), f32),
            v((8, HALF), f32),
            v((8, HALF), f32),
            v((8, HALF), f32),
            v((8, HALF), f32),
            v((RING, 1, HALF), f32),
            v((1, HALF), f32),
            v((1, HALF), f32),
            dma((2, 2)),
            dma((2, HOPS)),
            dma((2, 2, CUTS)),
            dma((2, HOPS - 2, CUTS)),
            dma((3, 2)),
            dma((3, 2)),
            dma((5,)),
            dma((5,)),
            dma((4,)),
            dma((4,)),
            dma((2,)),
            dma((2, 4)),
            pltpu.SemaphoreType.REGULAR,
            pltpu.SemaphoreType.REGULAR,
            pltpu.SemaphoreType.REGULAR,
            pltpu.SemaphoreType.REGULAR,
            dma((7,)),
        ],
        compiler_params=pltpu.CompilerParams(
            collective_id=0, has_side_effects=True, vmem_limit_bytes=48 * 2**20
        ),
        cost_estimate=pl.CostEstimate(
            flops=6 * ROWS * D * KV, bytes_accessed=8 * 2**20, transcendentals=ROWS
        ),
    )(*args)
    return pl.pallas_call(
        hand_over,
        out_shape=shapes,
        in_specs=[anywhere] * 6,
        out_specs=[hbm] * 6,
        scratch_shapes=[dma((6,))],
        compiler_params=pltpu.CompilerParams(vmem_limit_bytes=2**20),
    )(*[pltpu.with_memory_space_constraint(a, pltpu.VMEM) for a in outs])


def solution(mesh):
    placed = (
        P(("replica", "fsdp"), None),
        P("replica", None),
        P("replica", "fsdp", None),
        P(("replica", "fsdp"), None),
        P("replica", "fsdp", None),
        P("fsdp", None),
        P("fsdp", None),
    )
    return jax.shard_map(
        on_device,
        mesh=mesh,
        in_specs=placed,
        out_specs=(
            P(("replica", "fsdp"), None),
            P(("replica", "fsdp"), None),
            P("replica", "fsdp", None),
            P("replica", None),
            P("fsdp", None),
            P("fsdp", None),
        ),
        check_vma=False,
    )
```

```python
import functools

import jax
import jax.numpy as jnp
from jax import lax
from jax.experimental import pallas as pl
from jax.experimental.pallas import tpu as pltpu
from jax.sharding import PartitionSpec as P

eps = 1e-06
MESH = pl.DeviceIdType.MESH
f32, bf16 = jnp.float32, jnp.bfloat16

RING = 8
ROWS = 160
D = 4608
HALF = D // 2
KV = 1024
SHARD = 288
PIECE = SHARD // 2
HOPS = 7
CUTS = 1
CUT = PIECE // CUTS


def kernel(
    tok, gain, w, cot, frag, glob, mom,
    keys_o, gtok_o, gw_o, ggain_o, nglob_o, nmom_o,
    tokv, gainv, n2, nsend, c2, wall, part, rs_s, rs_r, dn_own, dn_s, dn_r, k_own, k_s, k_r,
    rstdv, fragv, globv, momv,
    nt, cn, pk_s, pk_r, zacc, zin_r, core_r, csum, xhi_r, ztotal, gring, gsum, gx_r,
    ag_ss, ag_rs, rs_ss, rs_rs, f_ss, f_rs, x_ss, x_rs, z_ss, z_rs, g_ss, g_rs, above_in, partner_in, core_in, xhi_in, loc,
):
    me = lax.axis_index("fsdp")
    rep = lax.axis_index("replica")
    x, y = me // RING, me % RING
    z, low = rep // 4, rep % 4
    core, xhi = low % 2, low // 2

    def fs(i):
        return {"fsdp": i}

    def rp(i):
        return {"replica": i}

    ring = (fs(x * RING + (y + 1) % RING), fs(x * RING + (y + RING - 1) % RING))
    last = RING - 1
    above, below = rp((z + 1) % RING * 4 + low), rp((z + last) % RING * 4 + low)
    partner = fs((1 - x) * RING + y)
    core_dev = rp(rep + 1 - 2 * core)
    xhi_dev = rp(rep + 2 - 4 * xhi)

    def local(i, src, dst):
        return pltpu.make_async_copy(src, dst, loc.at[i])

    def remote(src, dst, ss, rs, dev):
        return pltpu.make_async_remote_copy(
            src_ref=src, dst_ref=dst, send_sem=ss, recv_sem=rs, device_id=dev, device_id_type=MESH
        )

    own_rows = pl.ds(pl.multiple_of(y * SHARD, 16), SHARD)
    loads = [
        local(0, frag.at[0], fragv),
        local(1, tok, tokv),
        local(2, gain, gainv),
        local(3, cot, c2.at[pl.ds(0, ROWS)]),
        local(4, w.at[0], wall.at[own_rows]),
        local(5, glob, globv),
        local(6, mom, momv),
    ]

    barrier = pltpu.get_barrier_semaphore()

    def greet(peer):
        pl.semaphore_signal(barrier, inc=1, device_id=peer, device_id_type=MESH)

    for peer in ring:
        greet(peer)

    at_top = z == last
    pairs = (
        (True, x == 0, partner, partner_in),
        (at_top, core == 1, core_dev, core_in),
        (at_top, xhi == 0, xhi_dev, xhi_in),
    )

    @pl.when(z < last)
    def _():
        greet(above)

    greeted = 2 + jnp.where(z > 0, 1, 0)
    for member, earlier, peer, _ in pairs:
        pl.when(earlier & member)(functools.partial(greet, peer))
        greeted = greeted + jnp.where((~earlier) & member, 1, 0)
    pl.semaphore_wait(barrier, greeted)

    def tell(peer, sem):
        pl.semaphore_signal(sem, inc=1, device_id=peer, device_id_type=MESH)


    def know(pair):
        member, earlier, _, sem = pair
        pl.when(earlier & member)(lambda: pl.semaphore_wait(sem, 1))

    def wpiece(direction, j, extra):
        away = j // 2 + extra
        shard = (y + RING - away) % RING if direction == 0 else (y + away) % RING
        half = (j % 2) ^ direction
        return wall.at[pl.ds(pl.multiple_of(shard * SHARD + half * PIECE, 16), PIECE)]

    def ag_copy(direction, j):
        there = wpiece(direction, j, 0)
        half = (j % 2) ^ direction
        src = w.at[0, pl.ds(half * PIECE, PIECE)] if j < 2 else there
        return remote(src, there, ag_ss.at[direction, j % 2], ag_rs.at[direction, j], ring[direction])

    def ag_arrive(j):
        for direction in (0, 1):
            here = wpiece(direction, j, 1)
            remote(
                here, here, ag_ss.at[direction, j % 2], ag_rs.at[direction, j], ring[direction]
            ).wait_recv()
            if j + 2 < HOPS:
                ag_copy(direction, j).wait_send()
                ag_copy(direction, j + 2).start()

    for j in (0, 1):
        for direction in (0, 1):
            ag_copy(direction, j).start()

    for copy in loads:
        copy.start()
    pl.when(z > 0)(functools.partial(tell, below, above_in))
    for member, earlier, peer, sem in pairs:
        pl.when((~earlier) & member)(functools.partial(tell, peer, sem))

    x_c = remote(c2.at[pl.ds(0, ROWS)], c2.at[pl.ds(ROWS, ROWS)], x_ss.at[0], x_rs.at[0], partner)
    x_n = remote(nsend, n2.at[pl.ds(ROWS, ROWS)], x_ss.at[1], x_rs.at[1], partner)
    x_dn = remote(dn_s, dn_r, x_ss.at[2], x_rs.at[2], partner)
    x_k = remote(k_s, k_r, x_ss.at[3], x_rs.at[3], partner)
    x_g = remote(gsum, gx_r, x_ss.at[4], x_rs.at[4], partner)
    loads[3].wait()
    know(pairs[0])
    x_c.start()

    own, theirs = pl.ds(0, ROWS), pl.ds(ROWS, ROWS)

    def fc_copy(direction):
        return remote(
            c2.at[own], cn.at[direction, own],
            f_ss.at[0, direction], f_rs.at[0, direction], ring[direction],
        )

    def fx_copy(direction):
        return remote(
            cn.at[direction, own], cn.at[direction, theirs],
            f_ss.at[1, direction], f_rs.at[1, direction], partner,
        )

    def fn_copy(direction):
        return remote(
            pk_s.at[direction], pk_r.at[direction],
            f_ss.at[2, direction], f_rs.at[2, direction], ring[direction],
        )

    for direction in (0, 1):
        fc_copy(direction).start()

    def small_ring(buf, at, ss, rs, devs):
        def slot(direction, hop):
            return buf.at[(at + RING - hop) % RING if direction == 0 else (at + hop) % RING]

        def send(direction, hop):
            return remote(
                slot(direction, hop), slot(direction, hop),
                ss.at[direction], rs.at[direction, hop], devs[direction],
            )

        def arrive(hop):
            for direction in (0, 1):
                if hop < 4 - direction:
                    here = slot(direction, hop + 1)
                    remote(
                        here, here, ss.at[direction], rs.at[direction, hop], devs[direction]
                    ).wait_recv()
                    if hop + 1 < 4 - direction:
                        send(direction, hop).wait_send()
                        send(direction, hop + 1).start()

        return send, arrive

    g_send, g_arrive = small_ring(gring, y, g_ss, g_rs, ring)

    z_up = remote(zacc, zin_r, z_ss.at[0], z_rs.at[0], above)
    z_core = remote(zacc, core_r, z_ss.at[1], z_rs.at[1], core_dev)
    z_xhi = remote(csum, xhi_r, z_ss.at[2], z_rs.at[2], xhi_dev)
    z_down = remote(ztotal, ztotal, z_ss.at[3], z_rs.at[3], below)

    def z_rise(low, high):
        @pl.when((z >= low) & (z <= high))
        def _():
            if low > 0:
                z_up.wait_recv()
                zacc[...] = zacc[...] + zin_r[...]
            if high < last:
                pl.semaphore_wait(above_in, 1)
                z_up.start()

        if high == last:

            know(pairs[1])
            know(pairs[2])

            @pl.when(z == last)
            def _():
                z_core.start()

    def z_turn_core():
        @pl.when(z == last)
        def _():
            z_core.wait_recv()
            csum[...] = zacc[...] + core_r[...]
            z_xhi.start()

    def z_turn_x():
        @pl.when(z == last)
        def _():
            z_xhi.wait_recv()
            ztotal[...] = csum[...] + xhi_r[...]
            z_down.start()

    def z_fall(at):
        @pl.when(z == at)
        def _():
            z_down.wait_recv()
            if at > 0:
                z_down.start()

    loads[0].wait()
    zacc[pl.ds(0, 4), :] = fragv[:, pl.ds(0, HALF)].astype(f32)
    zacc[pl.ds(4, 4), :] = fragv[:, pl.ds(HALF, HALF)].astype(f32)

    loads[1].wait()
    loads[2].wait()
    mine = x * HALF
    other = (1 - x) * HALF
    step = 768

    def cols(base, at):
        return pl.ds(pl.multiple_of(base + at, 128), step)

    def norm_block(i, _):
        rows = pl.ds(pl.multiple_of(i * 16, 16), 16)
        total = jnp.zeros((16, 128), f32)
        for at in range(0, D, step):
            v = tokv[rows, pl.ds(at, step)].astype(f32)
            v = v * v
            for k in range(0, step, 128):
                total = total + v[:, k : k + 128]
        mean = jnp.sum(total, axis=-1, keepdims=True) * (1.0 / D)
        rstd = lax.rsqrt(mean + eps)
        rstdv[rows, :] = jnp.broadcast_to(rstd, (16, 128))
        for base, to in ((other, nsend), (mine, n2)):
            for at in range(0, HALF, step):
                unit = tokv[rows, cols(base, at)].astype(f32) * rstd
                to[rows, pl.ds(at, step)] = (unit * (1.0 + gainv[:, cols(base, at)])).astype(bf16)
        return 0

    lax.fori_loop(0, ROWS // 16, norm_block, 0)
    x_n.start()
    z_rise(0, 0)

    ag_arrive(0)
    z_rise(1, 2)
    ag_arrive(1)
    z_rise(3, 4)
    for direction in (0, 1):
        fc_copy(direction).wait_recv()
        fx_copy(direction).start()
    z_rise(5, 6)
    z_rise(7, 7)
    ag_arrive(2)
    z_turn_core()

    x_c.wait_recv()
    x_n.wait_recv()

    def part_block(i, _):
        at = pl.multiple_of(i * 256, 256)
        turned = n2[:, pl.ds(at, 256)].T
        nt[pl.ds(at, 256), :] = turned
        part[pl.ds(at, 256), :] = jnp.dot(turned, c2[...], preferred_element_type=f32)
        return 0

    lax.fori_loop(0, HALF // 256, part_block, 0)

    def part_rows(direction, away, half, cut):
        shard = (y + away) % RING if direction == 0 else (y + RING - away) % RING
        return pl.ds(pl.multiple_of(shard * SHARD + half * PIECE + cut * CUT, 16), CUT)

    def rs_copy(direction, j, cut):
        rows = pl.ds(cut * CUT, CUT)
        return remote(
            rs_s.at[direction, j, rows], rs_r.at[direction, j, rows],
            rs_ss.at[direction, j % 2, cut], rs_rs.at[direction, j - 2, cut], ring[direction],
        )

    def rs_send(direction, j, cut):
        half, away = (j % 2) ^ direction, 4 - (j + 1) // 2
        rows = pl.ds(cut * CUT, CUT)
        v = part[part_rows(direction, away, half, cut), :]
        if j >= 4:
            v = v + rs_r[direction, j - 2, rows, :].astype(f32)
        else:
            factor = (pk_r[direction, rows, pl.ds((j - 2) * 256, 256)], pk_r[direction, rows, pl.ds(512, 128)])
            zero = jnp.zeros((64, KV), bf16)
            rest = cn[direction, pl.ds(256, 64), :]
            rest = jnp.concatenate([rest, zero] if j == 2 else [zero, rest], axis=0)
            v = v + jnp.dot(factor[0], cn[direction, pl.ds(0, 256), :], preferred_element_type=f32)
            v = v + jnp.dot(factor[1], rest, preferred_element_type=f32)
        rs_s[direction, j, rows, :] = v.astype(bf16)
        if j >= 4:
            rs_copy(direction, j - 2, cut).wait_send()
        rs_copy(direction, j, cut).start()

    def rs_arrive(j):
        for direction in (0, 1):
            rs_copy(direction, j, 0).wait_recv()
        g_arrive(j - 2)
        for direction in (0, 1):
            rs_send(direction, j + 2, 0)

    def pack(direction):
        a, b = (nt[part_rows(direction, 4 - j, (j % 2) ^ direction, 0), :] for j in (0, 1))
        pk_s[direction, :, :] = jnp.concatenate(
            [a[:, :256], b[:, :256], a[:, 256:], b[:, 256:]], axis=1
        )
        fn_copy(direction).start()

    for direction in (0, 1):
        pack(direction)

    ag_arrive(3)
    z_turn_x()

    ag_arrive(4)
    z_fall(6)

    for direction in (0, 1):
        fn_copy(direction).wait_recv()
        fx_copy(direction).wait_recv()
        rs_send(direction, 2, 0)

    ag_arrive(5)
    z_fall(5)
    ag_arrive(6)
    z_fall(4)
    loads[4].wait()

    def dn_block(i, _):
        at = pl.multiple_of(i * 256, 256)
        v = lax.dot_general(
            c2[...], wall[pl.ds(at, 256), :], (((1,), (1,)), ((), ())), preferred_element_type=f32
        )
        dn_own[:, pl.ds(at, 256)] = v[:ROWS]
        dn_s[:, pl.ds(at, 256)] = v[ROWS:].astype(bf16)
        gring[y, :, pl.ds(at, 256)] = jnp.sum(
            v * n2[:, pl.ds(at, 256)].astype(f32), axis=0, keepdims=True
        )
        return 0

    lax.fori_loop(0, HALF // 256, dn_block, 0)
    x_dn.start()
    g_send(0, 0).start()
    g_send(1, 0).start()
    rs_send(0, 3, 0)
    rs_send(1, 3, 0)

    def key_block(i, _):
        at = pl.multiple_of(i * 256, 256)
        v = jnp.dot(n2[...], wall[:, pl.ds(at, 256)], preferred_element_type=f32)
        k_own[:, pl.ds(at, 256)] = v[:ROWS]
        k_s[:, pl.ds(at, 256)] = v[ROWS:].astype(bf16)
        return 0

    lax.fori_loop(0, KV // 256, key_block, 0)
    x_k.start()

    rs_arrive(2)
    z_fall(3)
    rs_arrive(3)
    z_fall(2)
    rs_arrive(4)
    z_fall(1)

    x_dn.wait_recv()

    def gtok_block(i, _):
        rows = pl.ds(pl.multiple_of(i * 16, 16), 16)
        rstd = rstdv[rows, pl.ds(0, 1)]
        total = jnp.zeros((16, 128), f32)
        for base, grad in ((mine, dn_own), (other, dn_r)):
            for at in range(0, HALF, step):
                unit = tokv[rows, cols(base, at)].astype(f32) * rstd
                scaled = grad[rows, pl.ds(at, step)].astype(f32) * (1.0 + gainv[:, cols(base, at)])
                v = scaled * unit
                for k in range(0, step, 128):
                    total = total + v[:, k : k + 128]
        mean = jnp.sum(total, axis=-1, keepdims=True) * (1.0 / D)
        for base, grad in ((mine, dn_own), (other, dn_r)):
            for at in range(0, HALF, step):
                unit = tokv[rows, cols(base, at)].astype(f32) * rstd
                scaled = grad[rows, pl.ds(at, step)].astype(f32) * (1.0 + gainv[:, cols(base, at)])
                gtok_o[rows, cols(base, at)] = (rstd * (scaled - unit * mean)).astype(bf16)
        return 0

    lax.fori_loop(0, ROWS // 16, gtok_block, 0)

    for cut in range(CUTS):
        for direction in (0, 1):
            rs_copy(direction, 5, cut).wait_recv()
            rows = part_rows(0, 0, 1 - direction, cut)
            part[rows, :] = part[rows, :] + rs_r[direction, 5, pl.ds(cut * CUT, CUT), :].astype(f32)
    z_fall(0)
    g_arrive(3)

    total = gring[0]
    for k in range(1, RING):
        total = total + gring[k]
    gsum[...] = total / (1.0 + gainv[:, pl.ds(pl.multiple_of(mine, 128), HALF)])
    x_g.start()

    loads[5].wait()
    loads[6].wait()
    for k in (0, 1):
        here = pl.ds(k * HALF, HALF)
        locals_sum = ztotal[pl.ds(4 * k, 4), :]
        g = globv[:, here]
        average = (32.0 * g - locals_sum) * (1.0 / 32.0)
        momentum = 0.9 * momv[:, here] + average
        nmom_o[:, here] = momentum
        nglob_o[:, here] = g - 0.7 * (average + 0.9 * momentum)

    x_k.wait_recv()

    def keys_block(i, _):
        rows = pl.ds(pl.multiple_of(i * 16, 16), 16)
        keys_o[rows, :] = (k_own[rows, :] + k_r[rows, :].astype(f32)).astype(bf16)
        return 0

    lax.fori_loop(0, ROWS // 16, keys_block, 0)

    for cut in range(CUTS):
        for direction in (0, 1):
            rs_copy(direction, 6, cut).wait_recv()
            v = part[part_rows(0, 0, direction, cut), :]
            v = v + rs_r[direction, 6, pl.ds(cut * CUT, CUT), :].astype(f32)
            gw_o[0, pl.ds(direction * PIECE + cut * CUT, CUT), :] = v.astype(bf16)

    x_g.wait_recv()
    ggain_o[:, pl.ds(pl.multiple_of(mine, 128), HALF)] = gsum[...]
    ggain_o[:, pl.ds(pl.multiple_of(other, 128), HALF)] = gx_r[...]

    for direction in (0, 1):
        for j in (HOPS - 2, HOPS - 1):
            ag_copy(direction, j).wait_send()
            for cut in range(CUTS):
                rs_copy(direction, j, cut).wait_send()
        for copy in (fc_copy, fx_copy, fn_copy):
            copy(direction).wait_send()
        g_send(direction, 3 - direction).wait_send()
    for copy in (x_c, x_n, x_dn, x_k, x_g):
        copy.wait_send()

    @pl.when(z < last)
    def _():
        z_up.wait_send()

    @pl.when(z == last)
    def _():
        z_core.wait_send()
        z_xhi.wait_send()

    @pl.when(z > 0)
    def _():
        z_down.wait_send()


def hand_over(*refs):
    sources, results, sems = refs[:6], refs[6:12], refs[12]
    copies = [
        pltpu.make_async_copy(src, dst, sems.at[i])
        for i, (src, dst) in enumerate(zip(sources, results))
    ]
    for copy in copies:
        copy.start()
    for copy in copies:
        copy.wait()


def on_device(tokens, gain, key_weight, key_cotangent, local_fragment, global_fragment, outer_momentum):
    v, dma = pltpu.VMEM, pltpu.SemaphoreType.DMA
    hbm, anywhere = pl.BlockSpec(memory_space=pltpu.HBM), pl.BlockSpec(memory_space=pl.ANY)
    shapes = (
        jax.ShapeDtypeStruct((ROWS, KV), bf16),
        jax.ShapeDtypeStruct((ROWS, D), bf16),
        jax.ShapeDtypeStruct((1, SHARD, KV), bf16),
        jax.ShapeDtypeStruct((1, D), f32),
        jax.ShapeDtypeStruct((4, D), f32),
        jax.ShapeDtypeStruct((4, D), f32),
    )
    args = (tokens, gain, key_weight, key_cotangent, local_fragment, global_fragment, outer_momentum)
    args = [pltpu.with_memory_space_constraint(a, pltpu.HBM) for a in args]
    outs = pl.pallas_call(
        kernel,
        out_shape=[v(s.shape, s.dtype) for s in shapes],
        in_specs=[hbm] * 7,
        out_specs=[pl.BlockSpec(memory_space=pltpu.VMEM)] * 6,
        scratch_shapes=[
            v((ROWS, D), bf16),
            v((1, D), f32),
            v((2 * ROWS, HALF), bf16),
            v((ROWS, HALF), bf16),
            v((2 * ROWS, KV), bf16),
            v((HALF, KV), bf16),
            v((HALF, KV), f32),
            v((2, HOPS, PIECE, KV), bf16),
            v((2, HOPS, PIECE, KV), bf16),
            v((ROWS, HALF), f32),
            v((ROWS, HALF), bf16),
            v((ROWS, HALF), bf16),
            v((ROWS, KV), f32),
            v((ROWS, KV), bf16),
            v((ROWS, KV), bf16),
            v((ROWS, 128), f32),
            v((4, D), bf16),
            v((4, D), f32),
            v((4, D), f32),
            v((HALF, 2 * ROWS), bf16),
            v((2, 2 * ROWS, KV), bf16),
            v((2, PIECE, 4 * ROWS), bf16),
            v((2, PIECE, 4 * ROWS), bf16),
            v((8, HALF), f32),
            v((8, HALF), f32),
            v((8, HALF), f32),
            v((8, HALF), f32),
            v((8, HALF), f32),
            v((8, HALF), f32),
            v((RING, 1, HALF), f32),
            v((1, HALF), f32),
            v((1, HALF), f32),
            dma((2, 2)),
            dma((2, HOPS)),
            dma((2, 2, CUTS)),
            dma((2, HOPS - 2, CUTS)),
            dma((3, 2)),
            dma((3, 2)),
            dma((5,)),
            dma((5,)),
            dma((4,)),
            dma((4,)),
            dma((2,)),
            dma((2, 4)),
            pltpu.SemaphoreType.REGULAR,
            pltpu.SemaphoreType.REGULAR,
            pltpu.SemaphoreType.REGULAR,
            pltpu.SemaphoreType.REGULAR,
            dma((7,)),
        ],
        compiler_params=pltpu.CompilerParams(
            collective_id=0, has_side_effects=True, vmem_limit_bytes=48 * 2**20
        ),
        cost_estimate=pl.CostEstimate(
            flops=6 * ROWS * D * KV, bytes_accessed=8 * 2**20, transcendentals=ROWS
        ),
    )(*args)
    return pl.pallas_call(
        hand_over,
        out_shape=shapes,
        in_specs=[anywhere] * 6,
        out_specs=[hbm] * 6,
        scratch_shapes=[dma((6,))],
        compiler_params=pltpu.CompilerParams(vmem_limit_bytes=2**20),
    )(*[pltpu.with_memory_space_constraint(a, pltpu.VMEM) for a in outs])


def solution(mesh):
    placed = (
        P(("replica", "fsdp"), None),
        P("replica", None),
        P("replica", "fsdp", None),
        P(("replica", "fsdp"), None),
        P("replica", "fsdp", None),
        P("fsdp", None),
        P("fsdp", None),
    )
    return jax.shard_map(
        on_device,
        mesh=mesh,
        in_specs=placed,
        out_specs=(
            P(("replica", "fsdp"), None),
            P(("replica", "fsdp"), None),
            P("replica", "fsdp", None),
            P("replica", None),
            P("fsdp", None),
            P("fsdp", None),
        ),
        check_vma=False,
    )
```
